128 devices in a mesh: clu: 16 (over y, z), smp: 8 (over x, core).
Axes of the slice: x: 4, y: 4, z: 4, core: 2. Of those that a mesh axis runs over, the one named last changes fastest.
Arguments:
- currents: float32 [4096, 2, 128], P(('clu', 'smp')), may hold values from -6 to 6
- near_blocks: bfloat16 [4096, 6, 2, 128, 128], P(('clu', 'smp')), may hold values from -0.15625 to 0.15625
- near_src: int32 [4096, 6], P(('clu', 'smp')), may hold values from 0 to 4095, as said below
- radiation: float32 [2, 128, 256], replicated, may hold values from -0.375 to 0.375
- interp: float32 [256, 1024], replicated, may hold values from -0.375 to 0.375
- shift_phase: float32 [8, 1024], replicated, may hold values from -3.140625 to 3.140625
- parent_map: int32 [16, 256], P('clu'), may hold values from 0 to 95, never falling along the last dimension, each value on 1 to 8 neighbouring positions
- octant: int32 [16, 256], P('clu'), may hold values from 0 to 7
- trans: float32 [316, 2, 1024], P(None, None, 'smp'), may hold values from -0.5 to 0.5
- far_src: int32 [1536, 64], P('clu'), may hold values from 0 to 1535, as said below
- far_kind: int32 [1536, 64], P('clu'), may hold values from 0 to 315, as said below
- receive: float32 [2, 256, 128], replicated, may hold values from -0.125 to 0.125
Outputs:
- product: float32 [4096, 2, 128], P(('clu', 'smp'))
The draws below stay inside these ranges and needn't reach their ends.
Inputs may be any that keep to these rules, and one draw needn't show every extreme that they name: near_src[l, 0] = l; every entry names a leaf held by the device that holds leaf l or by the device just before or after it in clu+smp order, and both neighbours are named wherever they exist. `parent_map`: numbers never fall along a row; every parent has 1 to 8 children and some parent of each group has exactly 8. `far_src`: the 64 entries of row t are distinct and name parents p with |p // 96 - t // 96| <= 1. far_kind[t, f] = (far_src[t, f] - t) mod 316.
All inputs are finite; a program needn't handle non-finite values.
Results may differ from the reference program's by a relative error of at most 0.0015.
Values may be sent and summed in bfloat16 or wider, within the bound.
A program may use at most 64 MiB of HBM per device.

```python
import math
import jax
import jax.numpy as jnp
import numpy as np
from jax import lax

UNK = 128
K1 = 256
K2 = 1024
NOPS = 316
NEAR = 6
FAR = 64
LEAF_DEV = 32
GROUP = 256
LEAVES = 4096
PAR_DEV = 96
PARENTS = 1536
N_CLU = 16
N_SMP = 8


def draw_near_src(key, part):
    key = jax.random.fold_in(key, 11)
    leaf_ids = jnp.arange(LEAVES, dtype=jnp.int32)
    first_ids = leaf_ids // LEAF_DEV * LEAF_DEV
    offsets = jax.random.randint(key, (LEAVES, NEAR - 3), -LEAF_DEV, 2 * LEAF_DEV, dtype=jnp.int32)
    random_cols = first_ids[:, None] + offsets
    before_col = (leaf_ids - LEAF_DEV)[:, None]
    after_col = (leaf_ids + LEAF_DEV)[:, None]
    columns = jnp.concatenate([leaf_ids[:, None], before_col, after_col, random_cols], axis=1)
    columns = jnp.where(columns < 0, columns + LEAF_DEV, columns)
    columns = jnp.where(columns >= LEAVES, columns - LEAF_DEV, columns)
    return columns.astype(jnp.int32)


def far_lists(key):
    key = jax.random.fold_in(key, 23)
    width = 3 * PAR_DEV
    targets = jnp.arange(PARENTS, dtype=jnp.int32)
    target_group = targets // PAR_DEV
    slots = jnp.arange(width, dtype=jnp.int32)
    cand_group = target_group[:, None] - 1 + (slots // PAR_DEV)[None, :]
    candidates = cand_group * PAR_DEV + (slots % PAR_DEV)[None, :]
    valid = (cand_group >= 0) & (cand_group < N_CLU)
    scores = jax.random.randint(key, (PARENTS, width), 0, 1 << 20, dtype=jnp.int32) * width + slots[None, :]
    scores = jnp.where(valid, scores, -1 - slots[None, :])
    _, picks = lax.top_k(scores, FAR)
    sources = jnp.take_along_axis(candidates, picks, axis=1).astype(jnp.int32)
    kinds = jnp.mod(sources - targets[:, None], NOPS).astype(jnp.int32)
    return (sources, kinds)


def draw_far_src(key, part):
    sources, kinds = far_lists(key)
    return sources


def draw_far_kind(key, part):
    sources, kinds = far_lists(key)
    return kinds


def set_ends(array, own_key, low, top_value):
    longest = array.shape.index(max(array.shape))
    spots = []
    for shift in (0, 1):
        where = [jax.random.randint(jax.random.fold_in(own_key, axis), (), 0, length) for axis, length in enumerate(array.shape)]
        where[longest] = (where[longest] + shift) % array.shape[longest]
        spots.append(tuple(where))
    return array.at[spots[0]].set(low).at[spots[1]].set(top_value)


def levels(rng, shape, cuts, least, largest):
    factor_of, own = 1.0, jax.random.fold_in(rng, 6)
    for dim, blocks in cuts:
        steps = jnp.exp(jax.random.uniform(jax.random.fold_in(own, dim), (blocks,), jnp.float32, least / len(cuts), largest / len(cuts)))
        factor_of = factor_of * jnp.repeat(steps, shape[dim] // blocks).reshape([-1 if axis == dim else 1 for axis in range(len(shape))])
    return factor_of


def length_profile(amount, total, most, lean):
    portions = [(1 << 20) // math.isqrt(rank ** lean) + 1 for rank in range(2, amount + 1)]
    surplus, counts = total - most - (amount - 1), [1] * (amount - 1)
    while surplus > 0:
        free = [i for i in range(amount - 1) if counts[i] < most]
        mass, remaining = sum([portions[i] for i in free]), surplus
        for i in free:
            more = min(most - counts[i], max(1, remaining * portions[i] // mass), surplus)
            counts[i] = counts[i] + more
            surplus = surplus - more
    return np.array([most] + counts)


def ragged(rng, amount, total, limit, lean):
    if amount == 2:
        one = jax.random.randint(rng, (), max(1, total - limit), min(limit, total - 1) + 1)
        return jnp.stack([one, total - one])
    sizes = jnp.asarray(length_profile(amount, total, limit, lean), jnp.int32)
    couples = (amount - 1) // 2
    donor, receiver = sizes[1:1 + 2 * couples:2], sizes[2:2 + 2 * couples:2]
    margin = jnp.minimum(donor - 1, limit - receiver)
    moved = jax.random.randint(jax.random.fold_in(rng, 1), (couples,), 0, 1 << 20) % (margin + 1)
    sizes = sizes.at[1:1 + 2 * couples:2].set(donor - moved).at[2:2 + 2 * couples:2].set(receiver + moved)
    return sizes[jax.random.permutation(jax.random.fold_in(rng, 2), amount)]


def noise(stream_key, dims, scale, bound, cuts=(), kind=jnp.bfloat16):
    values = scale * jax.random.normal(stream_key, dims, jnp.float32)
    if cuts:
        values = values * levels(stream_key, dims, cuts, -0.22, 0.18)
    return jnp.clip(values, -bound, bound).astype(kind)


def setup_inputs(seed: int = 0) -> dict:
    key_list = jax.random.split(jax.random.key(seed), 13)
    currents = noise(key_list[0], (LEAVES, 2, UNK), 1.0, 6.0, ((0, 128),), jnp.float32)
    near_blocks = noise(key_list[1], (LEAVES, NEAR, 2, UNK, UNK), (2 * NEAR * UNK) ** -0.5, 0.15625, ((0, 128),))
    near_src = draw_near_src(jax.random.fold_in(key_list[12], 71), 0)
    radiation = noise(key_list[3], (2, UNK, K1), (2 * UNK) ** -0.5, 0.375, (), jnp.float32)
    interp = noise(key_list[4], (K1, K2), K1 ** -0.5, 0.375, (), jnp.float32)
    shift_phase = jnp.clip(jax.random.uniform(key_list[5], (8, K2), jnp.float32, -3.140625, 3.140625), -3.140625, 3.140625)
    parent_map = jax.vmap(lambda own: jnp.searchsorted(jnp.cumsum(ragged(own, PAR_DEV, GROUP, 8, 1)), jnp.arange(GROUP), side="right"))(jax.random.split(key_list[6], N_CLU)).reshape((N_CLU, GROUP)).astype(jnp.int32)
    octant = set_ends(jax.random.randint(key_list[7], (N_CLU, GROUP), 0, 8), jax.random.fold_in(key_list[7], 1), 0, 7).astype(jnp.int32)
    trans = noise(key_list[8], (NOPS, 2, K2), (2 * FAR) ** -0.5, 0.5, ((2, 8),), jnp.float32)
    far_src = draw_far_src(jax.random.fold_in(key_list[12], 71), 0)
    far_kind = draw_far_kind(jax.random.fold_in(key_list[12], 71), 0)
    receive = noise(key_list[11], (2, K1, UNK), (8 * K1) ** -0.5, 0.125, (), jnp.float32)
    return dict(currents=currents, near_blocks=near_blocks, near_src=near_src, radiation=radiation, interp=interp, shift_phase=shift_phase, parent_map=parent_map, octant=octant, trans=trans, far_src=far_src, far_kind=far_kind, receive=receive)


highest = lax.Precision.HIGHEST


def complex_dot(left_real, left_imag, right_real, right_imag):
    real_part = jnp.dot(left_real, right_real, precision=highest, preferred_element_type=jnp.float32) - jnp.dot(left_imag, right_imag, precision=highest, preferred_element_type=jnp.float32)
    imag_part = jnp.dot(left_real, right_imag, precision=highest, preferred_element_type=jnp.float32) + jnp.dot(left_imag, right_real, precision=highest, preferred_element_type=jnp.float32)
    return real_part, imag_part


def near_part(operands):
    blocks, vectors = operands
    blocks = blocks.astype(jnp.float32)
    vectors = vectors.astype(jnp.float32)
    real_real = jnp.einsum('lsij,lsj->li', blocks[:, :, 0], vectors[:, :, 0])
    imag_imag = jnp.einsum('lsij,lsj->li', blocks[:, :, 1], vectors[:, :, 1])
    real_imag = jnp.einsum('lsij,lsj->li', blocks[:, :, 0], vectors[:, :, 1])
    imag_real = jnp.einsum('lsij,lsj->li', blocks[:, :, 1], vectors[:, :, 0])
    return jnp.stack([real_real - imag_imag, real_imag + imag_real], axis=1)


def reference(currents, near_blocks, near_src, radiation, interp, shift_phase, parent_map, octant, trans, far_src, far_kind, receive):
    devices_all = N_CLU * N_SMP
    near_currents = currents.astype(jnp.bfloat16)
    near_rows = near_currents[near_src]
    block_sets = near_blocks.reshape(devices_all, LEAF_DEV, NEAR, 2, UNK, UNK)
    row_sets = near_rows.reshape(devices_all, LEAF_DEV, NEAR, 2, UNK)
    near_field = lax.map(near_part, (block_sets, row_sets)).reshape(LEAVES, 2, UNK)

    pattern_real, pattern_imag = complex_dot(currents[:, 0], currents[:, 1], radiation[0], radiation[1])
    inter_real = jnp.dot(pattern_real, interp, precision=highest, preferred_element_type=jnp.float32)
    inter_imag = jnp.dot(pattern_imag, interp, precision=highest, preferred_element_type=jnp.float32)
    leaf_octant = octant.reshape(LEAVES)
    phase = shift_phase[leaf_octant]
    cos_rows = jnp.cos(phase)
    sin_rows = jnp.sin(phase)
    shifted_real = inter_real * cos_rows - inter_imag * sin_rows
    shifted_imag = inter_real * sin_rows + inter_imag * cos_rows
    owner = (parent_map + (jnp.arange(N_CLU, dtype=jnp.int32) * PAR_DEV)[:, None]).reshape(LEAVES).astype(jnp.int32)
    upper_real = jax.ops.segment_sum(shifted_real, owner, PARENTS)
    upper_imag = jax.ops.segment_sum(shifted_imag, owner, PARENTS)

    def translate(operands):
        sources, kinds = operands
        source_real = upper_real[sources]
        source_imag = upper_imag[sources]
        operators = trans[kinds]
        in_real = jnp.sum(operators[:, :, 0] * source_real - operators[:, :, 1] * source_imag, axis=1)
        in_imag = jnp.sum(operators[:, :, 0] * source_imag + operators[:, :, 1] * source_real, axis=1)
        return in_real, in_imag

    incoming_real, incoming_imag = lax.map(translate, (far_src.reshape(N_CLU, PAR_DEV, FAR), far_kind.reshape(N_CLU, PAR_DEV, FAR)))
    incoming_real = incoming_real.reshape(PARENTS, K2)
    incoming_imag = incoming_imag.reshape(PARENTS, K2)
    parent_real = incoming_real[owner]
    parent_imag = incoming_imag[owner]
    unshift_real = parent_real * cos_rows + parent_imag * sin_rows
    unshift_imag = parent_imag * cos_rows - parent_real * sin_rows
    spread_real = jnp.dot(unshift_real, interp.T, precision=highest, preferred_element_type=jnp.float32)
    spread_imag = jnp.dot(unshift_imag, interp.T, precision=highest, preferred_element_type=jnp.float32)
    far_real, far_imag = complex_dot(spread_real, spread_imag, receive[0], receive[1])
    return jnp.stack([near_field[:, 0] + far_real, near_field[:, 1] + far_imag], axis=1)
```

```python
import functools

import jax
import jax.numpy as jnp
from jax import lax
from jax.experimental import pallas as pl
from jax.experimental.pallas import tpu as pltpu
from jax.sharding import PartitionSpec as P

MESH = pl.DeviceIdType.MESH
F32 = jnp.float32
BF16 = jnp.bfloat16
I32 = jnp.int32
HIGHEST = lax.Precision.HIGHEST
NN = (((1,), (0,)), ((), ()))
NT = (((1,), (1,)), ((), ()))
TN = (((0,), (0,)), ((), ()))

CLU = 16
SMP = 8
LEAF = 32
GROUP = 256
PAR = 96
SLOTS = 6
KINDS = 316
TABLE = 384
BLOCKS = PAR // 8
WORDS = 9
CHUNK = 8
CHUNKS = LEAF // CHUNK
ORDER = (4, 3, 5, 2, 6, 1, 7)


def iota(shape, axis):
    return lax.broadcasted_iota(I32, shape, axis)


def mm(left, right, dims=NN, precision=None):
    return lax.dot_general(left, right, dims, precision=precision, preferred_element_type=F32)


def halves(value):
    high = value.astype(BF16)
    return high, (value - high.astype(F32)).astype(BF16)


def stacked(value):
    high, low = halves(value)
    return jnp.concatenate([high, low, high], axis=0)


def split3(value):
    high, low = halves(value)
    return jnp.concatenate([high, high, low], axis=1)


def complex_square(real, imag):
    return jnp.concatenate(
        [jnp.concatenate([real, imag], axis=1), jnp.concatenate([-imag, real], axis=1)], axis=0
    )


def far_masks(source):
    bits = jnp.left_shift(jnp.ones_like(source), source & 7).astype(F32)
    octet = lax.shift_right_logical(source, jnp.full_like(source, 3))
    rows = iota((40, PAR), 0)
    table = jnp.zeros((40, PAR), F32)
    for f in range(64):
        table = table + jnp.where(octet[f : f + 1] == rows, bits[f : f + 1], 0.0)
    flip = ((iota((PAR, PAR), 0) ^ 7) == iota((PAR, PAR), 1)).astype(BF16)
    table = jnp.concatenate([table, jnp.zeros((88, PAR), F32)], axis=0)
    octets = mm(flip, table.astype(BF16), NT).astype(I32)
    octets = jnp.left_shift(octets, 8 * (iota((PAR, 128), 1) & 3))
    pairs = octets + pltpu.roll(octets, 127, axis=1)
    return pairs + pltpu.roll(pairs, 126, axis=1)


def body(
    cur,
    blocks,
    near_src,
    rad,
    itp,
    phase,
    pmap,
    octant,
    trans,
    far_src,
    rec,
    out,
    xall,
    near_cur,
    near_blk,
    ns_v,
    rad_v,
    itp_v,
    ph_v,
    pm_v,
    oc_v,
    tr_v,
    fs_v,
    rec_v,
    t_re,
    t_im,
    upper,
    m_op,
    n_op,
    shift,
    to_parent,
    to_leaf,
    words,
    near_x,
    near_acc,
    part,
    arrived,
    load_sem,
    blk_sem,
    near_send,
    near_recv,
    cur_send,
    cur_recv,
    up_send,
    up_recv,
    part_send,
    part_recv,
):
    clu = lax.axis_index("clu")
    me = lax.axis_index("smp")
    device = clu * SMP + me
    after = lax.rem(device + 1, CLU * SMP)
    before = lax.rem(device + CLU * SMP - 1, CLU * SMP)
    after_id = (after // SMP, lax.rem(after, SMP))
    before_id = (before // SMP, lax.rem(before, SMP))
    up_id = (lax.rem(clu + 1, CLU), me)
    down_id = (lax.rem(clu + CLU - 1, CLU), me)
    peers = {o: (clu, lax.rem(me + o, SMP)) for o in range(1, SMP)}

    barrier = pltpu.get_barrier_semaphore()
    for where in (after_id, before_id, up_id, down_id, *peers.values()):
        pl.semaphore_signal(barrier, inc=1, device_id=where, device_id_type=MESH)

    columns = pl.ds(pl.multiple_of(me * 128, 128), 128)
    loads = [
        (cur, xall.at[me]),
        (itp.at[:, columns], itp_v),
        (phase.at[:, columns], ph_v),
        (rad, rad_v),
        (rec, rec_v),
        (pmap, pm_v),
        (octant, oc_v),
        (far_src, fs_v),
        (near_src, ns_v),
        (trans.at[pl.ds(KINDS - 192, 192)], tr_v.at[pl.ds(0, 192)]),
        (trans.at[pl.ds(0, 192)], tr_v.at[pl.ds(192, 192)]),
    ]
    copies = [
        pltpu.make_async_copy(source, target, load_sem.at[i])
        for i, (source, target) in enumerate(loads)
    ]
    for copy in copies:
        copy.start()
    blk_copies = [
        pltpu.make_async_copy(
            blocks.at[pl.ds(i * CHUNK, CHUNK)], near_blk.at[pl.ds(i * CHUNK, CHUNK)], blk_sem.at[i]
        )
        for i in range(CHUNKS)
    ]
    for copy in blk_copies:
        copy.start()

    copies[0].wait()
    near_cur[1, 0] = xall[me, :, 0, :].astype(BF16)
    near_cur[1, 1] = xall[me, :, 1, :].astype(BF16)

    pl.semaphore_wait(barrier, 4 + SMP - 1)
    near_out = [
        pltpu.make_async_remote_copy(
            src_ref=near_cur.at[1],
            dst_ref=near_cur.at[slot],
            send_sem=near_send.at[i],
            recv_sem=near_recv.at[i],
            device_id=where,
            device_id_type=MESH,
        )
        for i, (slot, where) in enumerate(((0, after_id), (2, before_id)))
    ]
    for copy in near_out:
        copy.start()
    cur_out = [
        pltpu.make_async_remote_copy(
            src_ref=xall.at[me],
            dst_ref=xall.at[me],
            send_sem=cur_send.at[o - 1],
            recv_sem=cur_recv.at[o - 1],
            device_id=peers[o],
            device_id_type=MESH,
        )
        for o in ORDER
    ]
    for copy in cur_out:
        copy.start()

    for copy in copies[1:9]:
        copy.wait()
    grid = itp_v[...]
    both = mm(rad_v[...].reshape(256, 256), grid, NN, HIGHEST)
    m_op[...] = stacked(complex_square(both[:128], both[128:]))
    both = mm(grid, jnp.concatenate([rec_v[0], rec_v[1]], axis=1), TN, HIGHEST)
    n_op[...] = stacked(complex_square(both[:, :128], both[:, 128:]))
    angles = ph_v[...]
    table = jnp.concatenate([jnp.cos(angles), jnp.sin(angles)], axis=1)
    position = (oc_v[...] == iota((8, GROUP), 0)).astype(F32)
    shift[...] = mm(position, table, TN, HIGHEST)
    owner = pm_v[...]
    member = (owner == iota((PAR, GROUP), 0)).astype(BF16)
    to_parent[...] = jnp.concatenate([member, member], axis=1)
    member = (owner == (iota((PAR, GROUP), 0) ^ 7)).astype(F32)
    to_leaf[...] = jnp.concatenate([member, member], axis=0).T.astype(BF16)
    masks = far_masks(fs_v[...] - (clu - 1) * PAR)
    for q in range(WORDS):
        words[q] = jnp.broadcast_to(masks[:, 4 * q : 4 * q + 1], (PAR, 128))
    copies[9].wait()
    copies[10].wait()
    t_re[...] = tr_v[:, 0, :]
    t_im[...] = tr_v[:, 1, :]

    for copy in near_out:
        copy.wait_recv()
    p_re = near_cur[:, 0].reshape(PAR, 128).astype(F32)
    p_im = near_cur[:, 1].reshape(PAR, 128).astype(F32)
    sources = jnp.concatenate(
        [jnp.concatenate([p_re, -p_im], axis=1), jnp.concatenate([p_im, p_re], axis=1)], axis=0
    )
    local = ns_v[...] - (device - 1) * LEAF
    local = jnp.concatenate(
        [local, local + PAR, jnp.full((SLOTS, 64), -1, I32)], axis=1
    )
    rows = iota((2 * PAR, 128), 0)
    picks = jnp.concatenate(
        [(local[s : s + 1] == rows).astype(F32) for s in range(SLOTS)], axis=1
    ).astype(BF16)
    rhs = mm(sources.T.astype(BF16), picks).astype(BF16)
    for s in range(SLOTS):
        near_x[pl.ds(s * 256, 256)] = rhs[:, s * 128 : (s + 1) * 128]

    lane_leaf = lax.rem(iota((128, 128), 1), LEAF)

    def near_chunk(i):
        blk_copies[i].wait()
        total = near_acc[...] if i else jnp.zeros((128, 128), F32)
        lhs = jnp.concatenate(
            [
                near_blk[pl.ds(i * CHUNK, CHUNK), s, c].reshape(CHUNK * 128, 128)
                for s in range(SLOTS)
                for c in range(2)
            ],
            axis=1,
        )
        result = mm(lhs, near_x[...])
        for r in range(CHUNK):
            total = jnp.where(
                lane_leaf == i * CHUNK + r, result[r * 128 : (r + 1) * 128], total
            )
        near_acc[...] = total

    for copy in cur_out:
        copy.wait_recv()
    x = jnp.concatenate(
        [xall[:, :, 0, :].reshape(GROUP, 128), xall[:, :, 1, :].reshape(GROUP, 128)], axis=1
    )
    inter = mm(split3(x), m_op[...])
    cos, sin = shift[:, :128], shift[:, 128:]
    real, imag = inter[:, :128], inter[:, 128:]
    shifted = jnp.concatenate([real * cos - imag * sin, real * sin + imag * cos], axis=1)
    own = mm(to_parent[...], jnp.concatenate(halves(shifted), axis=0))
    upper[1, 0] = own[:, :128]
    upper[1, 1] = own[:, 128:]
    up_out = [
        pltpu.make_async_remote_copy(
            src_ref=upper.at[1],
            dst_ref=upper.at[slot],
            send_sem=up_send.at[i],
            recv_sem=up_recv.at[i],
            device_id=where,
            device_id_type=MESH,
        )
        for i, (slot, where) in enumerate(((0, up_id), (2, down_id)))
    ]
    for copy in up_out:
        copy.start()

    def translate(group, sums):
        def word_step(turn, sums):
            word = 3 * group + turn

            def octet_step(step, sums):
                sums = list(sums)
                start = pl.multiple_of(32 * turn + 8 * step, 8)
                up_re = upper[group, 0, pl.ds(start, 8)]
                up_im = upper[group, 1, pl.ds(start, 8)]
                offset = jnp.full((8, 128), 8 * step, I32)
                marks = [
                    lax.shift_right_logical(words[word, 8 * b : 8 * b + 8], offset)
                    for b in range(BLOCKS)
                ]
                for i in range(8):
                    source_re = jnp.broadcast_to(up_re[i : i + 1], (8, 128))
                    source_im = jnp.broadcast_to(up_im[i : i + 1], (8, 128))
                    for b in range(BLOCKS):
                        at = 96 * group + start + (89 + i - 8 * b)
                        op_re = t_re[pl.ds(at, 8)]
                        op_im = t_im[pl.ds(at, 8)]
                        there = (marks[b] & (1 << i)) != 0
                        here_re = jnp.where(there, source_re, 0.0)
                        here_im = jnp.where(there, source_im, 0.0)
                        sums[2 * b] = sums[2 * b] + (op_re * here_re - op_im * here_im)
                        sums[2 * b + 1] = sums[2 * b + 1] + (op_re * here_im + op_im * here_re)
                return tuple(sums)

            return lax.fori_loop(0, 4, octet_step, sums)

        return lax.fori_loop(0, 3, word_step, sums)

    sums = tuple(jnp.zeros((8, 128), F32) for _ in range(2 * BLOCKS))
    sums = translate(1, sums)
    near_chunk(0)
    up_out[0].wait_recv()
    sums = translate(0, sums)
    up_out[1].wait_recv()
    sums = translate(2, sums)

    incoming = jnp.concatenate(
        [jnp.concatenate(sums[0::2], axis=0), jnp.concatenate(sums[1::2], axis=0)], axis=1
    )
    field = mm(to_leaf[...], jnp.concatenate(halves(incoming), axis=0))
    cos, sin = shift[:, :128], shift[:, 128:]
    real, imag = field[:, :128], field[:, 128:]
    back = jnp.concatenate([real * cos + imag * sin, imag * cos - real * sin], axis=1)
    part[...] = mm(split3(back), n_op[...]).reshape(SMP, LEAF, 256)
    part_out = [
        pltpu.make_async_remote_copy(
            src_ref=part.at[lax.rem(me + o, SMP)],
            dst_ref=arrived.at[o - 1],
            send_sem=part_send.at[o - 1],
            recv_sem=part_recv.at[o - 1],
            device_id=peers[o],
            device_id_type=MESH,
        )
        for o in ORDER
    ]
    for copy in part_out:
        copy.start()
    for i in range(1, CHUNKS):
        near_chunk(i)
    near = near_acc[...].T
    total = part[me] + jnp.concatenate([near[:LEAF], near[LEAF : 2 * LEAF]], axis=1)
    for copy, o in zip(part_out, ORDER):
        copy.wait_recv()
        total = total + arrived[o - 1]
    out[:, 0, :] = total[:, :128]
    out[:, 1, :] = total[:, 128:]
    for copy in (*near_out, *cur_out, *up_out, *part_out):
        copy.wait_send()


def on_device(
    currents,
    near_blocks,
    near_src,
    radiation,
    interp,
    shift_phase,
    parent_map,
    octant,
    trans,
    far_src,
    far_kind,
    receive,
):
    hbm_spec = pl.BlockSpec(memory_space=pltpu.HBM)
    vmem = pltpu.VMEM
    dma = pltpu.SemaphoreType.DMA
    return pl.pallas_call(
        body,
        out_shape=jax.ShapeDtypeStruct((LEAF, 2, 128), F32),
        in_specs=[hbm_spec] * 11,
        out_specs=pl.BlockSpec(memory_space=vmem),
        scratch_shapes=[
            vmem((SMP, LEAF, 2, 128), F32),
            vmem((3, 2, LEAF, 128), BF16),
            vmem((LEAF, SLOTS, 2, 128, 128), BF16),
            vmem((SLOTS, LEAF), I32),
            vmem((2, 128, 256), F32),
            vmem((256, 128), F32),
            vmem((8, 128), F32),
            vmem((1, GROUP), I32),
            vmem((1, GROUP), I32),
            vmem((TABLE, 2, 128), F32),
            vmem((64, PAR), I32),
            vmem((2, 256, 128), F32),
            vmem((TABLE, 128), F32),
            vmem((TABLE, 128), F32),
            vmem((3, 2, PAR, 128), F32),
            vmem((768, 256), BF16),
            vmem((768, 256), BF16),
            vmem((GROUP, 256), F32),
            vmem((PAR, 512), BF16),
            vmem((GROUP, 192), BF16),
            vmem((WORDS, PAR, 128), I32),
            vmem((SLOTS * 256, 128), BF16),
            vmem((128, 128), F32),
            vmem((SMP, LEAF, 256), F32),
            vmem((SMP - 1, LEAF, 256), F32),
            dma((11,)),
            dma((CHUNKS,)),
            dma((2,)),
            dma((2,)),
            dma((SMP - 1,)),
            dma((SMP - 1,)),
            dma((2,)),
            dma((2,)),
            dma((SMP - 1,)),
            dma((SMP - 1,)),
        ],
        compiler_params=pltpu.CompilerParams(
            collective_id=0, has_side_effects=True, vmem_limit_bytes=48 * 1024 * 1024
        ),
        name="far_and_near",
    )(
        currents,
        near_blocks,
        near_src.T,
        radiation,
        interp,
        shift_phase,
        parent_map,
        octant,
        trans,
        far_src.T,
        receive,
    )


def solution(mesh):
    in_specs = (
        P(("clu", "smp"), None, None),
        P(("clu", "smp"), None, None, None, None),
        P(("clu", "smp"), None),
        P(),
        P(),
        P(),
        P("clu", None),
        P("clu", None),
        P(None, None, "smp"),
        P("clu", None),
        P("clu", None),
        P(),
    )
    out_specs = P(("clu", "smp"), None, None)
    return jax.shard_map(
        on_device, mesh=mesh, in_specs=in_specs, out_specs=out_specs, check_vma=False
    )
```

```python
import functools

import jax
import jax.numpy as jnp
from jax import lax
from jax.experimental import pallas as pl
from jax.experimental.pallas import tpu as pltpu
from jax.sharding import PartitionSpec as P

MESH = pl.DeviceIdType.MESH
F32 = jnp.float32
BF16 = jnp.bfloat16
I32 = jnp.int32
HIGHEST = lax.Precision.HIGHEST
NN = (((1,), (0,)), ((), ()))
NT = (((1,), (1,)), ((), ()))
TN = (((0,), (0,)), ((), ()))

CLU = 16
SMP = 8
LEAF = 32
GROUP = 256
PAR = 96
SLOTS = 6
KINDS = 316
TABLE = 384
BLOCKS = PAR // 8
WORDS = 9
CHUNK = 8
CHUNKS = LEAF // CHUNK
ORDER = (4, 3, 5, 2, 6, 1, 7)


def iota(shape, axis):
    return lax.broadcasted_iota(I32, shape, axis)


def mm(left, right, dims=NN, precision=None):
    return lax.dot_general(left, right, dims, precision=precision, preferred_element_type=F32)


def halves(value):
    high = value.astype(BF16)
    return high, (value - high.astype(F32)).astype(BF16)


def stacked(value):
    high, low = halves(value)
    return jnp.concatenate([high, low, high], axis=0)


def split3(value):
    high, low = halves(value)
    return jnp.concatenate([high, high, low], axis=1)


def complex_square(real, imag):
    return jnp.concatenate(
        [jnp.concatenate([real, imag], axis=1), jnp.concatenate([-imag, real], axis=1)], axis=0
    )


def far_masks(source):
    bits = jnp.left_shift(jnp.ones_like(source), source & 7).astype(F32)
    octet = lax.shift_right_logical(source, jnp.full_like(source, 3))
    rows = iota((40, PAR), 0)
    table = jnp.zeros((40, PAR), F32)
    for f in range(64):
        table = table + jnp.where(octet[f : f + 1] == rows, bits[f : f + 1], 0.0)
    flip = ((iota((PAR, PAR), 0) ^ 7) == iota((PAR, PAR), 1)).astype(BF16)
    table = jnp.concatenate([table, jnp.zeros((88, PAR), F32)], axis=0)
    octets = mm(flip, table.astype(BF16), NT).astype(I32)
    octets = jnp.left_shift(octets, 8 * (iota((PAR, 128), 1) & 3))
    pairs = octets + pltpu.roll(octets, 127, axis=1)
    return pairs + pltpu.roll(pairs, 126, axis=1)


def body(
    cur,
    blocks,
    near_src,
    rad,
    itp,
    phase,
    pmap,
    octant,
    trans,
    far_src,
    rec,
    out,
    xall,
    near_cur,
    near_blk,
    ns_v,
    rad_v,
    itp_v,
    ph_v,
    pm_v,
    oc_v,
    tr_v,
    fs_v,
    rec_v,
    t_re,
    t_im,
    upper,
    m_op,
    n_op,
    shift,
    to_parent,
    to_leaf,
    words,
    near_x,
    near_acc,
    incoming,
    part,
    arrived,
    load_sem,
    blk_sem,
    near_send,
    near_recv,
    cur_send,
    cur_recv,
    up_send,
    up_recv,
    part_send,
    part_recv,
):
    clu = lax.axis_index("clu")
    me = lax.axis_index("smp")
    device = clu * SMP + me
    after = device + 1
    before = device + CLU * SMP - 1
    after_id = (lax.rem(after // SMP, CLU), lax.rem(after, SMP))
    before_id = (lax.rem(before // SMP, CLU), lax.rem(before, SMP))
    up_id = (lax.rem(clu + 1, CLU), me)
    down_id = (lax.rem(clu + CLU - 1, CLU), me)
    peers = {o: (clu, lax.rem(me + o, SMP)) for o in range(1, SMP)}
    has_after, has_before = device < CLU * SMP - 1, device > 0
    has_up, has_down = clu < CLU - 1, clu > 0

    barrier = pltpu.get_barrier_semaphore()

    def greet(where):
        pl.semaphore_signal(barrier, inc=1, device_id=where, device_id_type=MESH)

    greeted = SMP - 1
    for there, where in (
        (has_after, after_id),
        (has_before, before_id),
        (has_up, up_id),
        (has_down, down_id),
    ):
        pl.when(there)(functools.partial(greet, where))
        greeted = greeted + there.astype(I32)
    for where in peers.values():
        greet(where)

    columns = pl.ds(pl.multiple_of(me * 128, 128), 128)
    loads = [
        (cur, xall.at[me]),
        (itp.at[:, columns], itp_v),
        (phase.at[:, columns], ph_v),
        (rad, rad_v),
        (rec, rec_v),
        (pmap, pm_v),
        (octant, oc_v),
        (far_src, fs_v),
        (near_src, ns_v),
        (trans.at[pl.ds(KINDS - 192, 192)], tr_v.at[pl.ds(0, 192)]),
        (trans.at[pl.ds(0, 192)], tr_v.at[pl.ds(192, 192)]),
    ]
    copies = [
        pltpu.make_async_copy(source, target, load_sem.at[i])
        for i, (source, target) in enumerate(loads)
    ]
    for copy in copies:
        copy.start()
    blk_copies = [
        pltpu.make_async_copy(
            blocks.at[pl.ds(i * CHUNK, CHUNK)], near_blk.at[pl.ds(i * CHUNK, CHUNK)], blk_sem.at[i]
        )
        for i in range(CHUNKS)
    ]
    for copy in blk_copies:
        copy.start()

    copies[0].wait()
    near_cur[1, 0] = xall[me, :, 0, :].astype(BF16)
    near_cur[1, 1] = xall[me, :, 1, :].astype(BF16)

    def clear(near_slot, up_slot):
        if near_slot is not None:
            near_cur[near_slot] = jnp.zeros((2, LEAF, 128), BF16)
        if up_slot is not None:
            upper[up_slot] = jnp.zeros((2, PAR, 128), F32)

    pl.when(jnp.logical_not(has_before))(functools.partial(clear, 0, None))
    pl.when(jnp.logical_not(has_after))(functools.partial(clear, 2, None))
    pl.when(jnp.logical_not(has_down))(functools.partial(clear, None, 0))
    pl.when(jnp.logical_not(has_up))(functools.partial(clear, None, 2))
    pl.semaphore_wait(barrier, greeted)
    near_out = [
        pltpu.make_async_remote_copy(
            src_ref=near_cur.at[1],
            dst_ref=near_cur.at[slot],
            send_sem=near_send.at[i],
            recv_sem=near_recv.at[i],
            device_id=where,
            device_id_type=MESH,
        )
        for i, (slot, where) in enumerate(((0, after_id), (2, before_id)))
    ]
    for copy, there in zip(near_out, (has_after, has_before)):
        pl.when(there)(copy.start)
    cur_out = [
        pltpu.make_async_remote_copy(
            src_ref=xall.at[me],
            dst_ref=xall.at[me],
            send_sem=cur_send.at[o - 1],
            recv_sem=cur_recv.at[o - 1],
            device_id=peers[o],
            device_id_type=MESH,
        )
        for o in ORDER
    ]
    for copy in cur_out:
        copy.start()

    for copy in copies[1:9]:
        copy.wait()
    grid = itp_v[...]
    both = mm(split3(rad_v[...].reshape(256, 256)), stacked(grid))
    m_op[...] = stacked(complex_square(both[:128], both[128:]))
    both = mm(grid, jnp.concatenate([rec_v[0], rec_v[1]], axis=1), TN, HIGHEST)
    n_op[...] = stacked(complex_square(both[:, :128], both[:, 128:]))
    angles = ph_v[...]
    table = jnp.concatenate([jnp.cos(angles), jnp.sin(angles)], axis=1)
    position = (oc_v[...] == iota((8, GROUP), 0)).astype(F32)
    shift[...] = mm(position, table, TN, HIGHEST)
    owner = pm_v[...]
    member = (owner == iota((PAR, GROUP), 0)).astype(BF16)
    to_parent[...] = jnp.concatenate([member, member], axis=1)
    member = (owner == (iota((PAR, GROUP), 0) ^ 7)).astype(F32)
    to_leaf[...] = jnp.concatenate([member, member], axis=0).T.astype(BF16)
    masks = far_masks(fs_v[...] - (clu - 1) * PAR)
    for q in range(WORDS):
        words[q] = jnp.broadcast_to(masks[:, 4 * q : 4 * q + 1], (PAR, 128))
    copies[9].wait()
    copies[10].wait()
    t_re[...] = tr_v[:, 0, :]
    t_im[...] = tr_v[:, 1, :]

    for copy, there in zip(near_out, (has_before, has_after)):
        pl.when(there)(copy.wait_recv)
    p_re = near_cur[:, 0].reshape(PAR, 128).astype(F32)
    p_im = near_cur[:, 1].reshape(PAR, 128).astype(F32)
    sources = jnp.concatenate(
        [jnp.concatenate([p_re, -p_im], axis=1), jnp.concatenate([p_im, p_re], axis=1)], axis=0
    )
    local = ns_v[...] - (device - 1) * LEAF
    local = jnp.concatenate(
        [local, local + PAR, jnp.full((SLOTS, 64), -1, I32)], axis=1
    )
    rows = iota((2 * PAR, 128), 0)
    picks = jnp.concatenate(
        [(local[s : s + 1] == rows).astype(F32) for s in range(SLOTS)], axis=1
    ).astype(BF16)
    rhs = mm(sources.T.astype(BF16), picks).astype(BF16)
    for s in range(SLOTS):
        near_x[pl.ds(s * 256, 256)] = rhs[:, s * 128 : (s + 1) * 128]

    lane_leaf = lax.rem(iota((128, 128), 1), LEAF)

    def near_chunk(i, carry):
        first = pl.multiple_of(i * CHUNK, CHUNK)
        pltpu.make_async_copy(
            blocks.at[pl.ds(first, CHUNK)], near_blk.at[pl.ds(first, CHUNK)], blk_sem.at[i]
        ).wait()
        lhs = jnp.concatenate(
            [
                near_blk[pl.ds(first, CHUNK), s, c].reshape(CHUNK * 128, 128)
                for s in range(SLOTS)
                for c in range(2)
            ],
            axis=1,
        )
        result = mm(lhs, near_x[...])
        total = near_acc[...]
        for r in range(CHUNK):
            total = jnp.where(lane_leaf == first + r, result[r * 128 : (r + 1) * 128], total)
        near_acc[...] = total
        return carry

    for copy in cur_out:
        copy.wait_recv()
    x = jnp.concatenate(
        [xall[:, :, 0, :].reshape(GROUP, 128), xall[:, :, 1, :].reshape(GROUP, 128)], axis=1
    )
    inter = mm(split3(x), m_op[...])
    cos, sin = shift[:, :128], shift[:, 128:]
    real, imag = inter[:, :128], inter[:, 128:]
    shifted = jnp.concatenate([real * cos - imag * sin, real * sin + imag * cos], axis=1)
    own = mm(to_parent[...], jnp.concatenate(halves(shifted), axis=0))
    upper[1, 0] = own[:, :128]
    upper[1, 1] = own[:, 128:]
    up_out = [
        pltpu.make_async_remote_copy(
            src_ref=upper.at[1],
            dst_ref=upper.at[slot],
            send_sem=up_send.at[i],
            recv_sem=up_recv.at[i],
            device_id=where,
            device_id_type=MESH,
        )
        for i, (slot, where) in enumerate(((0, up_id), (2, down_id)))
    ]
    for copy, there in zip(up_out, (has_up, has_down)):
        pl.when(there)(copy.start)

    def translate(group):
        def octet_step(step, sums):
            sums = list(sums)
            start = pl.multiple_of(8 * step, 8)
            up_re = upper[group, 0, pl.ds(start, 8)]
            up_im = upper[group, 1, pl.ds(start, 8)]
            offset = jnp.full((8, 128), 8 * lax.rem(step, 4), I32)
            word = 3 * group + step // 4
            marks = [
                lax.shift_right_logical(words[word, 8 * b : 8 * b + 8], offset)
                for b in range(BLOCKS)
            ]
            for i in range(8):
                source_re = jnp.broadcast_to(up_re[i : i + 1], (8, 128))
                source_im = jnp.broadcast_to(up_im[i : i + 1], (8, 128))
                for b in range(BLOCKS):
                    at = PAR * group + start + (89 + i - 8 * b)
                    op_re = t_re[pl.ds(at, 8)]
                    op_im = t_im[pl.ds(at, 8)]
                    there = (marks[b] & (1 << i)) != 0
                    here_re = jnp.where(there, source_re, 0.0)
                    here_im = jnp.where(there, source_im, 0.0)
                    sums[2 * b] = sums[2 * b] + (op_re * here_re - op_im * here_im)
                    sums[2 * b + 1] = sums[2 * b + 1] + (op_re * here_im + op_im * here_re)
            return tuple(sums)

        sums = tuple(
            incoming[8 * b : 8 * b + 8, 128 * c : 128 * c + 128]
            for b in range(BLOCKS)
            for c in range(2)
        )
        sums = lax.fori_loop(0, BLOCKS, octet_step, sums)
        for b in range(BLOCKS):
            for c in range(2):
                incoming[8 * b : 8 * b + 8, 128 * c : 128 * c + 128] = sums[2 * b + c]

    part_out = [
        pltpu.make_async_remote_copy(
            src_ref=part.at[lax.rem(me + o, SMP)],
            dst_ref=arrived.at[o - 1],
            send_sem=part_send.at[o - 1],
            recv_sem=part_recv.at[o - 1],
            device_id=peers[o],
            device_id_type=MESH,
        )
        for o in ORDER
    ]

    def spread():
        field = mm(to_leaf[...], jnp.concatenate(halves(incoming[...]), axis=0))
        cos, sin = shift[:, :128], shift[:, 128:]
        real, imag = field[:, :128], field[:, 128:]
        back = jnp.concatenate([real * cos + imag * sin, imag * cos - real * sin], axis=1)
        part[...] = mm(split3(back), n_op[...]).reshape(SMP, LEAF, 256)
        for copy in part_out:
            copy.start()

    incoming[...] = jnp.zeros((PAR, 256), F32)
    near_acc[...] = jnp.zeros((128, 128), F32)

    order = jnp.where(lax.rem(clu, 4) == 0, 1, 2)

    def phase(turn, carry):
        group = lax.rem(1 + order * turn, 3)
        pl.when((group == 0) & has_down)(up_out[0].wait_recv)
        pl.when((group == 2) & has_up)(up_out[1].wait_recv)
        translate(group)
        pl.when(turn == 2)(spread)
        lax.fori_loop(
            jnp.minimum(turn, 1), jnp.where(turn == 2, CHUNKS, 1), near_chunk, 0
        )
        return carry

    lax.fori_loop(0, 3, phase, 0)
    near = near_acc[...].T
    total = part[me] + jnp.concatenate([near[:LEAF], near[LEAF : 2 * LEAF]], axis=1)
    for copy, o in zip(part_out, ORDER):
        copy.wait_recv()
        total = total + arrived[o - 1]
    out[:, 0, :] = total[:, :128]
    out[:, 1, :] = total[:, 128:]
    for copy, there in zip((*near_out, *up_out), (has_after, has_before, has_up, has_down)):
        pl.when(there)(copy.wait_send)
    for copy in (*cur_out, *part_out):
        copy.wait_send()


def on_device(
    currents,
    near_blocks,
    near_src,
    radiation,
    interp,
    shift_phase,
    parent_map,
    octant,
    trans,
    far_src,
    far_kind,
    receive,
):
    hbm_spec = pl.BlockSpec(memory_space=pltpu.HBM)
    vmem = pltpu.VMEM
    dma = pltpu.SemaphoreType.DMA
    return pl.pallas_call(
        body,
        out_shape=vmem((LEAF, 2, 128), F32),
        in_specs=[hbm_spec] * 11,
        out_specs=pl.BlockSpec(memory_space=vmem),
        scratch_shapes=[
            vmem((SMP, LEAF, 2, 128), F32),
            vmem((3, 2, LEAF, 128), BF16),
            vmem((LEAF, SLOTS, 2, 128, 128), BF16),
            vmem((SLOTS, LEAF), I32),
            vmem((2, 128, 256), F32),
            vmem((256, 128), F32),
            vmem((8, 128), F32),
            vmem((1, GROUP), I32),
            vmem((1, GROUP), I32),
            vmem((TABLE, 2, 128), F32),
            vmem((64, PAR), I32),
            vmem((2, 256, 128), F32),
            vmem((TABLE, 128), F32),
            vmem((TABLE, 128), F32),
            vmem((3, 2, PAR, 128), F32),
            vmem((768, 256), BF16),
            vmem((768, 256), BF16),
            vmem((GROUP, 256), F32),
            vmem((PAR, 512), BF16),
            vmem((GROUP, 192), BF16),
            vmem((WORDS, PAR, 128), I32),
            vmem((SLOTS * 256, 128), BF16),
            vmem((128, 128), F32),
            vmem((PAR, 256), F32),
            vmem((SMP, LEAF, 256), F32),
            vmem((SMP - 1, LEAF, 256), F32),
            dma((11,)),
            dma((CHUNKS,)),
            dma((2,)),
            dma((2,)),
            dma((SMP - 1,)),
            dma((SMP - 1,)),
            dma((2,)),
            dma((2,)),
            dma((SMP - 1,)),
            dma((SMP - 1,)),
        ],
        compiler_params=pltpu.CompilerParams(
            collective_id=0, has_side_effects=True, vmem_limit_bytes=60 * 1024 * 1024
        ),
        name="far_and_near",
    )(
        currents,
        near_blocks,
        near_src.T,
        radiation,
        interp,
        shift_phase,
        parent_map,
        octant,
        trans,
        far_src.T,
        receive,
    )


def solution(mesh):
    in_specs = (
        P(("clu", "smp"), None, None),
        P(("clu", "smp"), None, None, None, None),
        P(("clu", "smp"), None),
        P(),
        P(),
        P(),
        P("clu", None),
        P("clu", None),
        P(None, None, "smp"),
        P("clu", None),
        P("clu", None),
        P(),
    )
    out_specs = P(("clu", "smp"), None, None)
    return jax.shard_map(
        on_device, mesh=mesh, in_specs=in_specs, out_specs=out_specs, check_vma=False
    )
```

```python
import functools

import jax
import jax.numpy as jnp
from jax import lax
from jax.experimental import pallas as pl
from jax.experimental.pallas import tpu as pltpu
from jax.sharding import PartitionSpec as P

MESH = pl.DeviceIdType.MESH
F32 = jnp.float32
BF16 = jnp.bfloat16
I32 = jnp.int32
HIGHEST = lax.Precision.HIGHEST
NN = (((1,), (0,)), ((), ()))
NT = (((1,), (1,)), ((), ()))
TN = (((0,), (0,)), ((), ()))

CLU = 16
SMP = 8
LEAF = 32
GROUP = 256
PAR = 96
SLOTS = 6
KINDS = 316
TABLE = 384
BLOCKS = PAR // 8
WORDS = 9
CHUNK = 8
CHUNKS = LEAF // CHUNK
STEPS = 32000.0
ORDER = (4, 3, 5, 2, 6, 1, 7)


def iota(shape, axis):
    return lax.broadcasted_iota(I32, shape, axis)


def mm(left, right, dims=NN, precision=None):
    return lax.dot_general(left, right, dims, precision=precision, preferred_element_type=F32)


def halves(value):
    high = value.astype(BF16)
    return high, (value - high.astype(F32)).astype(BF16)


def stacked(value):
    high, low = halves(value)
    return jnp.concatenate([high, low, high], axis=0)


def split3(value):
    high, low = halves(value)
    return jnp.concatenate([high, high, low], axis=1)


def coded(value):
    top = jnp.maximum(jnp.max(jnp.abs(value), axis=0, keepdims=True), 1e-30)
    power = jnp.ceil(jnp.log2(top))
    whole = jnp.floor(value * (STEPS * jnp.exp2(-power)) + 0.5)
    return whole.astype(I32), power


def message(parts):
    pairs = [coded(part) for part in parts]
    tail = [jnp.broadcast_to(power, (8, 128)).astype(I32) for _, power in pairs]
    return jnp.concatenate([whole for whole, _ in pairs] + tail, axis=0).astype(jnp.int16)


def decoded(block, rows):
    value = block.astype(I32).astype(F32)
    scale = [
        jnp.exp2(value[2 * rows + 8 * c : 2 * rows + 8 * c + 1]) * (1.0 / STEPS) for c in range(2)
    ]
    return [value[c * rows : (c + 1) * rows] * scale[c] for c in range(2)]


def complex_square(real, imag):
    return jnp.concatenate(
        [jnp.concatenate([real, imag], axis=1), jnp.concatenate([-imag, real], axis=1)], axis=0
    )


def far_masks(source):
    bits = jnp.left_shift(jnp.ones_like(source), source & 7).astype(F32)
    octet = lax.shift_right_logical(source, jnp.full_like(source, 3))
    rows = iota((40, PAR), 0)
    table = jnp.zeros((40, PAR), F32)
    for f in range(64):
        table = table + jnp.where(octet[f : f + 1] == rows, bits[f : f + 1], 0.0)
    flip = ((iota((PAR, PAR), 0) ^ 7) == iota((PAR, PAR), 1)).astype(BF16)
    table = jnp.concatenate([table, jnp.zeros((88, PAR), F32)], axis=0)
    octets = mm(flip, table.astype(BF16), NT).astype(I32)
    octets = jnp.left_shift(octets, 8 * (iota((PAR, 128), 1) & 3))
    pairs = octets + pltpu.roll(octets, 127, axis=1)
    return pairs + pltpu.roll(pairs, 126, axis=1)


def body(
    cur,
    blocks,
    near_src,
    rad,
    itp,
    phase,
    pmap,
    octant,
    trans,
    far_src,
    rec,
    out,
    cur_v,
    cur_msg,
    near_cur,
    near_blk,
    ns_v,
    rad_v,
    itp_v,
    ph_v,
    pm_v,
    oc_v,
    tr_v,
    fs_v,
    rec_v,
    t_re,
    t_im,
    upper,
    up_msg,
    m_op,
    n_op,
    shift,
    to_parent,
    to_leaf,
    words,
    near_x,
    near_acc,
    incoming,
    part,
    part_msg,
    arrived,
    load_sem,
    blk_sem,
    near_send,
    near_recv,
    cur_send,
    cur_recv,
    up_send,
    up_recv,
    part_send,
    part_recv,
):
    clu = lax.axis_index("clu")
    me = lax.axis_index("smp")
    device = clu * SMP + me
    after = device + 1
    before = device + CLU * SMP - 1
    after_id = (lax.rem(after // SMP, CLU), lax.rem(after, SMP))
    before_id = (lax.rem(before // SMP, CLU), lax.rem(before, SMP))
    up_id = (lax.rem(clu + 1, CLU), me)
    down_id = (lax.rem(clu + CLU - 1, CLU), me)
    peers = {o: (clu, lax.rem(me + o, SMP)) for o in range(1, SMP)}
    has_after, has_before = device < CLU * SMP - 1, device > 0
    has_up, has_down = clu < CLU - 1, clu > 0

    barrier = pltpu.get_barrier_semaphore()

    def greet(where):
        pl.semaphore_signal(barrier, inc=1, device_id=where, device_id_type=MESH)

    greeted = SMP - 1
    for there, where in (
        (has_after, after_id),
        (has_before, before_id),
        (has_up, up_id),
        (has_down, down_id),
    ):
        pl.when(there)(functools.partial(greet, where))
        greeted = greeted + there.astype(I32)
    for where in peers.values():
        greet(where)

    columns = pl.ds(pl.multiple_of(me * 128, 128), 128)
    loads = [
        (cur, cur_v),
        (itp.at[:, columns], itp_v),
        (phase.at[:, columns], ph_v),
        (rad, rad_v),
        (rec, rec_v),
        (pmap, pm_v),
        (octant, oc_v),
        (far_src, fs_v),
        (near_src, ns_v),
        (trans.at[pl.ds(KINDS - 192, 192)], tr_v.at[pl.ds(0, 192)]),
        (trans.at[pl.ds(0, 192)], tr_v.at[pl.ds(192, 192)]),
    ]
    copies = [
        pltpu.make_async_copy(source, target, load_sem.at[i])
        for i, (source, target) in enumerate(loads)
    ]
    for copy in copies:
        copy.start()
    blk_copies = [
        pltpu.make_async_copy(
            blocks.at[pl.ds(i * CHUNK, CHUNK)], near_blk.at[pl.ds(i * CHUNK, CHUNK)], blk_sem.at[i]
        )
        for i in range(CHUNKS)
    ]
    for copy in blk_copies:
        copy.start()

    copies[0].wait()
    own_cur = [cur_v[:, c, :] for c in range(2)]
    for c in range(2):
        near_cur[1, c] = own_cur[c].astype(BF16)
    cur_msg[me] = message(own_cur)

    def clear(near_slot, up_slot):
        if near_slot is not None:
            near_cur[near_slot] = jnp.zeros((2, LEAF, 128), BF16)
        if up_slot is not None:
            up_msg[up_slot] = jnp.zeros((2 * PAR + 16, 128), jnp.int16)

    pl.when(jnp.logical_not(has_before))(functools.partial(clear, 0, None))
    pl.when(jnp.logical_not(has_after))(functools.partial(clear, 2, None))
    pl.when(jnp.logical_not(has_down))(functools.partial(clear, None, 0))
    pl.when(jnp.logical_not(has_up))(functools.partial(clear, None, 2))
    pl.semaphore_wait(barrier, greeted)
    near_out = [
        pltpu.make_async_remote_copy(
            src_ref=near_cur.at[1],
            dst_ref=near_cur.at[slot],
            send_sem=near_send.at[i],
            recv_sem=near_recv.at[i],
            device_id=where,
            device_id_type=MESH,
        )
        for i, (slot, where) in enumerate(((0, after_id), (2, before_id)))
    ]
    cur_out = [
        pltpu.make_async_remote_copy(
            src_ref=cur_msg.at[me],
            dst_ref=cur_msg.at[me],
            send_sem=cur_send.at[o - 1],
            recv_sem=cur_recv.at[o - 1],
            device_id=peers[o],
            device_id_type=MESH,
        )
        for o in ORDER
    ]
    for copy in cur_out:
        copy.start()
    for copy, there in zip(near_out, (has_after, has_before)):
        pl.when(there)(copy.start)

    for copy in copies[1:9]:
        copy.wait()
    grid = itp_v[...]
    both = mm(split3(rad_v[...].reshape(256, 256)), stacked(grid))
    m_op[...] = stacked(complex_square(both[:128], both[128:]))
    both = mm(grid, jnp.concatenate([rec_v[0], rec_v[1]], axis=1), TN, HIGHEST)
    n_op[...] = stacked(complex_square(both[:, :128], both[:, 128:]))
    angles = ph_v[...]
    table = jnp.concatenate([jnp.cos(angles), jnp.sin(angles)], axis=1)
    position = (oc_v[...] == iota((8, GROUP), 0)).astype(F32)
    shift[...] = mm(position, table, TN, HIGHEST)
    owner = pm_v[...]
    member = (owner == iota((PAR, GROUP), 0)).astype(BF16)
    to_parent[...] = jnp.concatenate([member, member], axis=1)
    member = (owner == (iota((PAR, GROUP), 0) ^ 7)).astype(F32)
    to_leaf[...] = jnp.concatenate([member, member], axis=0).T.astype(BF16)
    masks = far_masks(fs_v[...] - (clu - 1) * PAR)
    for q in range(WORDS):
        words[q] = jnp.broadcast_to(masks[:, 4 * q : 4 * q + 1], (PAR, 128))
    copies[9].wait()
    copies[10].wait()
    t_re[...] = tr_v[:, 0, :]
    t_im[...] = tr_v[:, 1, :]

    lane_leaf = lax.rem(iota((128, 128), 1), LEAF)

    def near_chunk(i, carry):
        first = pl.multiple_of(i * CHUNK, CHUNK)
        pltpu.make_async_copy(
            blocks.at[pl.ds(first, CHUNK)], near_blk.at[pl.ds(first, CHUNK)], blk_sem.at[i]
        ).wait()
        lhs = jnp.concatenate(
            [
                near_blk[pl.ds(first, CHUNK), s, c].reshape(CHUNK * 128, 128)
                for s in range(SLOTS)
                for c in range(2)
            ],
            axis=1,
        )
        result = mm(lhs, near_x[...])
        total = near_acc[...]
        for r in range(CHUNK):
            total = jnp.where(lane_leaf == first + r, result[r * 128 : (r + 1) * 128], total)
        near_acc[...] = total
        return carry

    for copy in cur_out:
        copy.wait_recv()
    x = jnp.concatenate(
        [jnp.concatenate(decoded(cur_msg[i], LEAF), axis=1) for i in range(SMP)], axis=0
    )
    inter = mm(split3(x), m_op[...])
    cos, sin = shift[:, :128], shift[:, 128:]
    real, imag = inter[:, :128], inter[:, 128:]
    shifted = jnp.concatenate([real * cos - imag * sin, real * sin + imag * cos], axis=1)
    own = mm(to_parent[...], jnp.concatenate(halves(shifted), axis=0))
    own = [own[:, :128], own[:, 128:]]
    for c in range(2):
        upper[1, c] = own[c]
    up_msg[1] = message(own)
    up_out = [
        pltpu.make_async_remote_copy(
            src_ref=up_msg.at[1],
            dst_ref=up_msg.at[slot],
            send_sem=up_send.at[i],
            recv_sem=up_recv.at[i],
            device_id=where,
            device_id_type=MESH,
        )
        for i, (slot, where) in enumerate(((0, up_id), (2, down_id)))
    ]
    for copy, there in zip(up_out, (has_up, has_down)):
        pl.when(there)(copy.start)

    for copy, there in zip(near_out, (has_before, has_after)):
        pl.when(there)(copy.wait_recv)
    p_re = near_cur[:, 0].reshape(PAR, 128).astype(F32)
    p_im = near_cur[:, 1].reshape(PAR, 128).astype(F32)
    sources = jnp.concatenate(
        [jnp.concatenate([p_re, -p_im], axis=1), jnp.concatenate([p_im, p_re], axis=1)], axis=0
    )
    local = ns_v[...] - (device - 1) * LEAF
    local = jnp.concatenate(
        [local, local + PAR, jnp.full((SLOTS, 64), -1, I32)], axis=1
    )
    rows = iota((2 * PAR, 128), 0)
    picks = jnp.concatenate(
        [(local[s : s + 1] == rows).astype(F32) for s in range(SLOTS)], axis=1
    ).astype(BF16)
    rhs = mm(sources.T.astype(BF16), picks).astype(BF16)
    for s in range(SLOTS):
        near_x[pl.ds(s * 256, 256)] = rhs[:, s * 128 : (s + 1) * 128]

    def translate(group):
        def octet_step(step, sums):
            sums = list(sums)
            start = pl.multiple_of(8 * step, 8)
            up_re = upper[group, 0, pl.ds(start, 8)]
            up_im = upper[group, 1, pl.ds(start, 8)]
            offset = jnp.full((8, 128), 8 * lax.rem(step, 4), I32)
            word = 3 * group + step // 4
            marks = [
                lax.shift_right_logical(words[word, 8 * b : 8 * b + 8], offset)
                for b in range(BLOCKS)
            ]
            for i in range(8):
                source_re = jnp.broadcast_to(up_re[i : i + 1], (8, 128))
                source_im = jnp.broadcast_to(up_im[i : i + 1], (8, 128))
                for b in range(BLOCKS):
                    at = PAR * group + start + (89 + i - 8 * b)
                    op_re = t_re[pl.ds(at, 8)]
                    op_im = t_im[pl.ds(at, 8)]
                    there = (marks[b] & (1 << i)) != 0
                    here_re = jnp.where(there, source_re, 0.0)
                    here_im = jnp.where(there, source_im, 0.0)
                    sums[2 * b] = sums[2 * b] + (op_re * here_re - op_im * here_im)
                    sums[2 * b + 1] = sums[2 * b + 1] + (op_re * here_im + op_im * here_re)
            return tuple(sums)

        sums = tuple(
            incoming[8 * b : 8 * b + 8, 128 * c : 128 * c + 128]
            for b in range(BLOCKS)
            for c in range(2)
        )
        sums = lax.fori_loop(0, BLOCKS, octet_step, sums)
        for b in range(BLOCKS):
            for c in range(2):
                incoming[8 * b : 8 * b + 8, 128 * c : 128 * c + 128] = sums[2 * b + c]

    part_out = [
        pltpu.make_async_remote_copy(
            src_ref=part_msg.at[lax.rem(me + o, SMP)],
            dst_ref=arrived.at[o - 1],
            send_sem=part_send.at[o - 1],
            recv_sem=part_recv.at[o - 1],
            device_id=peers[o],
            device_id_type=MESH,
        )
        for o in ORDER
    ]

    def spread():
        field = mm(to_leaf[...], jnp.concatenate(halves(incoming[...]), axis=0))
        cos, sin = shift[:, :128], shift[:, 128:]
        real, imag = field[:, :128], field[:, 128:]
        back = jnp.concatenate([real * cos + imag * sin, imag * cos - real * sin], axis=1)
        result = mm(split3(back), n_op[...])
        part[...] = result.reshape(SMP, LEAF, 256)
        for i in range(SMP):
            rows = result[i * LEAF : (i + 1) * LEAF]
            part_msg[i] = message([rows[:, :128], rows[:, 128:]])
        for copy in part_out:
            copy.start()

    incoming[...] = jnp.zeros((PAR, 256), F32)
    near_acc[...] = jnp.zeros((128, 128), F32)

    order = jnp.where(lax.rem(clu, 4) == 0, 1, 2)

    def phase(turn, carry):
        group = lax.rem(1 + order * turn, 3)
        pl.when((group == 0) & has_down)(up_out[0].wait_recv)
        pl.when((group == 2) & has_up)(up_out[1].wait_recv)

        @pl.when(turn > 0)
        def take():
            for c, value in enumerate(decoded(up_msg[group], PAR)):
                upper[group, c] = value

        translate(group)
        pl.when(turn == 2)(spread)
        lax.fori_loop(
            jnp.minimum(turn, 1), jnp.where(turn == 2, CHUNKS, 1), near_chunk, 0
        )
        return carry

    lax.fori_loop(0, 3, phase, 0)
    near = near_acc[...].T
    total = part[me] + jnp.concatenate([near[:LEAF], near[LEAF : 2 * LEAF]], axis=1)
    for copy, o in zip(part_out, ORDER):
        copy.wait_recv()
        total = total + jnp.concatenate(decoded(arrived[o - 1], LEAF), axis=1)
    out[:, 0, :] = total[:, :128]
    out[:, 1, :] = total[:, 128:]
    for copy, there in zip((*near_out, *up_out), (has_after, has_before, has_up, has_down)):
        pl.when(there)(copy.wait_send)
    for copy in (*cur_out, *part_out):
        copy.wait_send()


def on_device(
    currents,
    near_blocks,
    near_src,
    radiation,
    interp,
    shift_phase,
    parent_map,
    octant,
    trans,
    far_src,
    far_kind,
    receive,
):
    hbm_spec = pl.BlockSpec(memory_space=pltpu.HBM)
    vmem = pltpu.VMEM
    dma = pltpu.SemaphoreType.DMA
    return pl.pallas_call(
        body,
        out_shape=vmem((LEAF, 2, 128), F32),
        in_specs=[hbm_spec] * 11,
        out_specs=pl.BlockSpec(memory_space=vmem),
        scratch_shapes=[
            vmem((LEAF, 2, 128), F32),
            vmem((SMP, 2 * LEAF + 16, 128), jnp.int16),
            vmem((3, 2, LEAF, 128), BF16),
            vmem((LEAF, SLOTS, 2, 128, 128), BF16),
            vmem((SLOTS, LEAF), I32),
            vmem((2, 128, 256), F32),
            vmem((256, 128), F32),
            vmem((8, 128), F32),
            vmem((1, GROUP), I32),
            vmem((1, GROUP), I32),
            vmem((TABLE, 2, 128), F32),
            vmem((64, PAR), I32),
            vmem((2, 256, 128), F32),
            vmem((TABLE, 128), F32),
            vmem((TABLE, 128), F32),
            vmem((3, 2, PAR, 128), F32),
            vmem((3, 2 * PAR + 16, 128), jnp.int16),
            vmem((768, 256), BF16),
            vmem((768, 256), BF16),
            vmem((GROUP, 256), F32),
            vmem((PAR, 512), BF16),
            vmem((GROUP, 192), BF16),
            vmem((WORDS, PAR, 128), I32),
            vmem((SLOTS * 256, 128), BF16),
            vmem((128, 128), F32),
            vmem((PAR, 256), F32),
            vmem((SMP, LEAF, 256), F32),
            vmem((SMP, 2 * LEAF + 16, 128), jnp.int16),
            vmem((SMP - 1, 2 * LEAF + 16, 128), jnp.int16),
            dma((11,)),
            dma((CHUNKS,)),
            dma((2,)),
            dma((2,)),
            dma((SMP - 1,)),
            dma((SMP - 1,)),
            dma((2,)),
            dma((2,)),
            dma((SMP - 1,)),
            dma((SMP - 1,)),
        ],
        compiler_params=pltpu.CompilerParams(
            collective_id=0, has_side_effects=True, vmem_limit_bytes=60 * 1024 * 1024
        ),
        name="far_and_near",
    )(
        currents,
        near_blocks,
        near_src.T,
        radiation,
        interp,
        shift_phase,
        parent_map,
        octant,
        trans,
        far_src.T,
        receive,
    )


def solution(mesh):
    in_specs = (
        P(("clu", "smp"), None, None),
        P(("clu", "smp"), None, None, None, None),
        P(("clu", "smp"), None),
        P(),
        P(),
        P(),
        P("clu", None),
        P("clu", None),
        P(None, None, "smp"),
        P("clu", None),
        P("clu", None),
        P(),
    )
    out_specs = P(("clu", "smp"), None, None)
    return jax.shard_map(
        on_device, mesh=mesh, in_specs=in_specs, out_specs=out_specs, check_vma=False
    )
```

```python
import functools

import jax
import jax.numpy as jnp
from jax import lax
from jax.experimental import pallas as pl
from jax.experimental.pallas import tpu as pltpu
from jax.sharding import PartitionSpec as P

MESH = pl.DeviceIdType.MESH
F32 = jnp.float32
BF16 = jnp.bfloat16
I32 = jnp.int32
HIGHEST = lax.Precision.HIGHEST
NN = (((1,), (0,)), ((), ()))
NT = (((1,), (1,)), ((), ()))
TN = (((0,), (0,)), ((), ()))

CLU = 16
SMP = 8
LEAF = 32
GROUP = 256
PAR = 96
SLOTS = 6
KINDS = 316
TABLE = 384
BLOCKS = PAR // 8
WORDS = 9
CHUNK = 8
CHUNKS = LEAF // CHUNK
STEPS = 32000.0
ORDER = (4, 3, 5, 2, 6, 1, 7)


def iota(shape, axis):
    return lax.broadcasted_iota(I32, shape, axis)


def mm(left, right, dims=NN, precision=None):
    return lax.dot_general(left, right, dims, precision=precision, preferred_element_type=F32)


def halves(value):
    high = value.astype(BF16)
    return high, (value - high.astype(F32)).astype(BF16)


def stacked(value):
    high, low = halves(value)
    return jnp.concatenate([high, low, high], axis=0)


def split3(value):
    high, low = halves(value)
    return jnp.concatenate([high, high, low], axis=1)


def coded(value):
    top = jnp.maximum(jnp.max(jnp.abs(value), axis=0, keepdims=True), 1e-30)
    power = jnp.ceil(jnp.log2(top))
    whole = jnp.floor(value * (STEPS * jnp.exp2(-power)) + 0.5)
    return whole.astype(I32), power


def message(parts):
    pairs = [coded(part) for part in parts]
    tail = [jnp.broadcast_to(power, (8, 128)).astype(I32) for _, power in pairs]
    return jnp.concatenate([whole for whole, _ in pairs] + tail, axis=0).astype(jnp.int16)


def decoded(block, rows):
    value = block.astype(I32).astype(F32)
    scale = [
        jnp.exp2(value[2 * rows + 8 * c : 2 * rows + 8 * c + 1]) * (1.0 / STEPS) for c in range(2)
    ]
    return [value[c * rows : (c + 1) * rows] * scale[c] for c in range(2)]


def complex_square(real, imag):
    return jnp.concatenate(
        [jnp.concatenate([real, imag], axis=1), jnp.concatenate([-imag, real], axis=1)], axis=0
    )


def far_masks(source):
    bits = jnp.left_shift(jnp.ones_like(source), source & 7).astype(F32)
    octet = lax.shift_right_logical(source, jnp.full_like(source, 3))
    rows = iota((40, PAR), 0)
    table = jnp.zeros((40, PAR), F32)
    for f in range(64):
        table = table + jnp.where(octet[f : f + 1] == rows, bits[f : f + 1], 0.0)
    flip = ((iota((PAR, PAR), 0) ^ 7) == iota((PAR, PAR), 1)).astype(BF16)
    table = jnp.concatenate([table, jnp.zeros((88, PAR), F32)], axis=0)
    octets = mm(flip, table.astype(BF16), NT).astype(I32)
    octets = jnp.left_shift(octets, 8 * (iota((PAR, 128), 1) & 3))
    pairs = octets + pltpu.roll(octets, 127, axis=1)
    return pairs + pltpu.roll(pairs, 126, axis=1)


def body(
    cur,
    blocks,
    near_src,
    rad,
    itp,
    phase,
    pmap,
    octant,
    trans,
    far_src,
    rec,
    out,
    cur_v,
    cur_msg,
    near_cur,
    near_blk,
    ns_v,
    rad_v,
    itp_v,
    ph_v,
    pm_v,
    oc_v,
    tr_v,
    fs_v,
    rec_v,
    t_re,
    t_im,
    upper,
    up_msg,
    m_op,
    n_op,
    shift,
    to_parent,
    to_leaf,
    words,
    near_x,
    near_acc,
    incoming,
    part,
    part_msg,
    arrived,
    load_sem,
    blk_sem,
    near_send,
    near_recv,
    cur_send,
    cur_recv,
    up_send,
    up_recv,
    part_send,
    part_recv,
    up_greet,
    near_greet,
):
    clu = lax.axis_index("clu")
    me = lax.axis_index("smp")
    device = clu * SMP + me
    after = device + 1
    before = device + CLU * SMP - 1
    after_id = (lax.rem(after // SMP, CLU), lax.rem(after, SMP))
    before_id = (lax.rem(before // SMP, CLU), lax.rem(before, SMP))
    up_id = (lax.rem(clu + 1, CLU), me)
    down_id = (lax.rem(clu + CLU - 1, CLU), me)
    peers = {o: (clu, lax.rem(me + o, SMP)) for o in range(1, SMP)}
    has_after, has_before = device < CLU * SMP - 1, device > 0
    has_up, has_down = clu < CLU - 1, clu > 0

    barrier = pltpu.get_barrier_semaphore()

    def greet(where):
        pl.semaphore_signal(barrier, inc=1, device_id=where, device_id_type=MESH)

    defers = (lax.rem(clu, 4) == 0) & has_down
    late = (lax.rem(clu, 4) == 3) & has_up
    near_defers = defers & (me == 0)
    near_late = late & (me == SMP - 1)

    greeted = SMP - 1
    for to, from_, where in (
        (has_after & jnp.logical_not(near_late), has_after, after_id),
        (has_before, has_before & jnp.logical_not(near_defers), before_id),
        (has_up & jnp.logical_not(late), has_up, up_id),
        (has_down, has_down & jnp.logical_not(defers), down_id),
    ):
        pl.when(to)(functools.partial(greet, where))
        greeted = greeted + from_.astype(I32)
    for where in peers.values():
        greet(where)

    columns = pl.ds(pl.multiple_of(me * 128, 128), 128)
    loads = [
        (cur, cur_v),
        (itp.at[:, columns], itp_v),
        (phase.at[:, columns], ph_v),
        (rad, rad_v),
        (rec, rec_v),
        (pmap, pm_v),
        (octant, oc_v),
        (far_src, fs_v),
        (near_src, ns_v),
        (trans.at[pl.ds(KINDS - 192, 192)], tr_v.at[pl.ds(0, 192)]),
        (trans.at[pl.ds(0, 192)], tr_v.at[pl.ds(192, 192)]),
    ]
    copies = [
        pltpu.make_async_copy(source, target, load_sem.at[i])
        for i, (source, target) in enumerate(loads)
    ]
    for copy in copies:
        copy.start()
    blk_copies = [
        pltpu.make_async_copy(
            blocks.at[pl.ds(i * CHUNK, CHUNK)], near_blk.at[pl.ds(i * CHUNK, CHUNK)], blk_sem.at[i]
        )
        for i in range(CHUNKS)
    ]
    for copy in blk_copies:
        copy.start()

    copies[0].wait()
    own_cur = [cur_v[:, c, :] for c in range(2)]
    for c in range(2):
        near_cur[1, c] = own_cur[c].astype(BF16)
    cur_msg[me] = message(own_cur)

    def clear(near_slot, up_slot):
        if near_slot is not None:
            near_cur[near_slot] = jnp.zeros((2, LEAF, 128), BF16)
        if up_slot is not None:
            up_msg[up_slot] = jnp.zeros((2 * PAR + 16, 128), jnp.int16)

    pl.when(jnp.logical_not(has_before))(functools.partial(clear, 0, None))
    pl.when(jnp.logical_not(has_after))(functools.partial(clear, 2, None))
    pl.when(jnp.logical_not(has_down))(functools.partial(clear, None, 0))
    pl.when(jnp.logical_not(has_up))(functools.partial(clear, None, 2))
    pl.semaphore_wait(barrier, greeted)

    def called(there, semaphore, where):
        @pl.when(there)
        def call():
            pl.semaphore_signal(semaphore, inc=1, device_id=where, device_id_type=MESH)

    called(late, up_greet, up_id)
    called(near_late, near_greet, after_id)
    near_out = [
        pltpu.make_async_remote_copy(
            src_ref=near_cur.at[1],
            dst_ref=near_cur.at[slot],
            send_sem=near_send.at[i],
            recv_sem=near_recv.at[i],
            device_id=where,
            device_id_type=MESH,
        )
        for i, (slot, where) in enumerate(((0, after_id), (2, before_id)))
    ]
    cur_out = [
        pltpu.make_async_remote_copy(
            src_ref=cur_msg.at[me],
            dst_ref=cur_msg.at[me],
            send_sem=cur_send.at[o - 1],
            recv_sem=cur_recv.at[o - 1],
            device_id=peers[o],
            device_id_type=MESH,
        )
        for o in ORDER
    ]
    for copy in cur_out:
        copy.start()
    for copy, there in zip(near_out, (has_after, has_before & jnp.logical_not(near_defers))):
        pl.when(there)(copy.start)

    for copy in copies[1:9]:
        copy.wait()
    grid = itp_v[...]
    both = mm(split3(rad_v[...].reshape(256, 256)), stacked(grid))
    m_op[...] = stacked(complex_square(both[:128], both[128:]))
    both = mm(grid, jnp.concatenate([rec_v[0], rec_v[1]], axis=1), TN, HIGHEST)
    n_op[...] = stacked(complex_square(both[:, :128], both[:, 128:]))
    angles = ph_v[...]
    table = jnp.concatenate([jnp.cos(angles), jnp.sin(angles)], axis=1)
    position = (oc_v[...] == iota((8, GROUP), 0)).astype(F32)
    shift[...] = mm(position, table, TN, HIGHEST)
    owner = pm_v[...]
    member = (owner == iota((PAR, GROUP), 0)).astype(BF16)
    to_parent[...] = jnp.concatenate([member, member], axis=1)
    member = (owner == (iota((PAR, GROUP), 0) ^ 7)).astype(F32)
    to_leaf[...] = jnp.concatenate([member, member], axis=0).T.astype(BF16)
    masks = far_masks(fs_v[...] - (clu - 1) * PAR)
    for q in range(WORDS):
        words[q] = jnp.broadcast_to(masks[:, 4 * q : 4 * q + 1], (PAR, 128))
    copies[9].wait()
    copies[10].wait()
    t_re[...] = tr_v[:, 0, :]
    t_im[...] = tr_v[:, 1, :]

    lane_leaf = lax.rem(iota((128, 128), 1), LEAF)

    def near_chunk(i, carry):
        first = pl.multiple_of(i * CHUNK, CHUNK)
        pltpu.make_async_copy(
            blocks.at[pl.ds(first, CHUNK)], near_blk.at[pl.ds(first, CHUNK)], blk_sem.at[i]
        ).wait()
        lhs = jnp.concatenate(
            [
                near_blk[pl.ds(first, CHUNK), s, c].reshape(CHUNK * 128, 128)
                for s in range(SLOTS)
                for c in range(2)
            ],
            axis=1,
        )
        result = mm(lhs, near_x[...])
        total = near_acc[...]
        for r in range(CHUNK):
            total = jnp.where(lane_leaf == first + r, result[r * 128 : (r + 1) * 128], total)
        near_acc[...] = total
        return carry

    for copy in cur_out:
        copy.wait_recv()
    x = jnp.concatenate(
        [jnp.concatenate(decoded(cur_msg[i], LEAF), axis=1) for i in range(SMP)], axis=0
    )
    inter = mm(split3(x), m_op[...])
    cos, sin = shift[:, :128], shift[:, 128:]
    real, imag = inter[:, :128], inter[:, 128:]
    shifted = jnp.concatenate([real * cos - imag * sin, real * sin + imag * cos], axis=1)
    own = mm(to_parent[...], jnp.concatenate(halves(shifted), axis=0))
    own = [own[:, :128], own[:, 128:]]
    for c in range(2):
        upper[1, c] = own[c]
    up_msg[1] = message(own)
    up_out = [
        pltpu.make_async_remote_copy(
            src_ref=up_msg.at[1],
            dst_ref=up_msg.at[slot],
            send_sem=up_send.at[i],
            recv_sem=up_recv.at[i],
            device_id=where,
            device_id_type=MESH,
        )
        for i, (slot, where) in enumerate(((0, up_id), (2, down_id)))
    ]
    pl.when(has_up)(up_out[0].start)

    @pl.when(defers)
    def await_late():
        pl.semaphore_wait(up_greet, 1)

    pl.when(has_down)(up_out[1].start)

    @pl.when(near_defers)
    def await_near_late():
        pl.semaphore_wait(near_greet, 1)
        near_out[1].start()

    def translate(group):
        def octet_step(step, sums):
            sums = list(sums)
            start = pl.multiple_of(8 * step, 8)
            up_re = upper[group, 0, pl.ds(start, 8)]
            up_im = upper[group, 1, pl.ds(start, 8)]
            offset = jnp.full((8, 128), 8 * lax.rem(step, 4), I32)
            word = 3 * group + step // 4
            marks = [
                lax.shift_right_logical(words[word, 8 * b : 8 * b + 8], offset)
                for b in range(BLOCKS)
            ]
            for i in range(8):
                source_re = jnp.broadcast_to(up_re[i : i + 1], (8, 128))
                source_im = jnp.broadcast_to(up_im[i : i + 1], (8, 128))
                for b in range(BLOCKS):
                    at = PAR * group + start + (89 + i - 8 * b)
                    op_re = t_re[pl.ds(at, 8)]
                    op_im = t_im[pl.ds(at, 8)]
                    there = (marks[b] & (1 << i)) != 0
                    here_re = jnp.where(there, source_re, 0.0)
                    here_im = jnp.where(there, source_im, 0.0)
                    sums[2 * b] = sums[2 * b] + (op_re * here_re - op_im * here_im)
                    sums[2 * b + 1] = sums[2 * b + 1] + (op_re * here_im + op_im * here_re)
            return tuple(sums)

        sums = tuple(
            incoming[8 * b : 8 * b + 8, 128 * c : 128 * c + 128]
            for b in range(BLOCKS)
            for c in range(2)
        )
        sums = lax.fori_loop(0, BLOCKS, octet_step, sums)
        for b in range(BLOCKS):
            for c in range(2):
                incoming[8 * b : 8 * b + 8, 128 * c : 128 * c + 128] = sums[2 * b + c]

    part_out = [
        pltpu.make_async_remote_copy(
            src_ref=part_msg.at[lax.rem(me + o, SMP)],
            dst_ref=arrived.at[o - 1],
            send_sem=part_send.at[o - 1],
            recv_sem=part_recv.at[o - 1],
            device_id=peers[o],
            device_id_type=MESH,
        )
        for o in ORDER
    ]

    def spread():
        field = mm(to_leaf[...], jnp.concatenate(halves(incoming[...]), axis=0))
        cos, sin = shift[:, :128], shift[:, 128:]
        real, imag = field[:, :128], field[:, 128:]
        back = jnp.concatenate([real * cos + imag * sin, imag * cos - real * sin], axis=1)
        result = mm(split3(back), n_op[...])
        part[...] = result.reshape(SMP, LEAF, 256)
        for i in range(SMP):
            rows = result[i * LEAF : (i + 1) * LEAF]
            part_msg[i] = message([rows[:, :128], rows[:, 128:]])
        for copy in part_out:
            copy.start()

    incoming[...] = jnp.zeros((PAR, 256), F32)
    near_acc[...] = jnp.zeros((128, 128), F32)

    order = jnp.where(lax.rem(clu, 4) == 0, 1, 2)

    def phase(turn, carry):
        group = lax.rem(1 + order * turn, 3)
        pl.when((group == 0) & has_down)(up_out[0].wait_recv)
        pl.when((group == 2) & has_up)(up_out[1].wait_recv)

        @pl.when(turn > 0)
        def take():
            for c, value in enumerate(decoded(up_msg[group], PAR)):
                upper[group, c] = value

        translate(group)
        pl.when(turn == 2)(spread)
        return carry

    lax.fori_loop(0, 3, phase, 0)

    for copy, there in zip(near_out, (has_before, has_after)):
        pl.when(there)(copy.wait_recv)
    p_re = near_cur[:, 0].reshape(PAR, 128).astype(F32)
    p_im = near_cur[:, 1].reshape(PAR, 128).astype(F32)
    sources = jnp.concatenate(
        [jnp.concatenate([p_re, -p_im], axis=1), jnp.concatenate([p_im, p_re], axis=1)], axis=0
    )
    local = ns_v[...] - (device - 1) * LEAF
    local = jnp.concatenate(
        [local, local + PAR, jnp.full((SLOTS, 64), -1, I32)], axis=1
    )
    rows = iota((2 * PAR, 128), 0)
    picks = jnp.concatenate(
        [(local[s : s + 1] == rows).astype(F32) for s in range(SLOTS)], axis=1
    ).astype(BF16)
    rhs = mm(sources.T.astype(BF16), picks).astype(BF16)
    for s in range(SLOTS):
        near_x[pl.ds(s * 256, 256)] = rhs[:, s * 128 : (s + 1) * 128]

    lax.fori_loop(0, CHUNKS, near_chunk, 0)
    near = near_acc[...].T
    total = part[me] + jnp.concatenate([near[:LEAF], near[LEAF : 2 * LEAF]], axis=1)
    for copy, o in zip(part_out, ORDER):
        copy.wait_recv()
        total = total + jnp.concatenate(decoded(arrived[o - 1], LEAF), axis=1)
    out[:, 0, :] = total[:, :128]
    out[:, 1, :] = total[:, 128:]
    for copy, there in zip((*near_out, *up_out), (has_after, has_before, has_up, has_down)):
        pl.when(there)(copy.wait_send)
    for copy in (*cur_out, *part_out):
        copy.wait_send()


def on_device(
    currents,
    near_blocks,
    near_src,
    radiation,
    interp,
    shift_phase,
    parent_map,
    octant,
    trans,
    far_src,
    far_kind,
    receive,
):
    hbm_spec = pl.BlockSpec(memory_space=pltpu.HBM)
    vmem = pltpu.VMEM
    dma = pltpu.SemaphoreType.DMA
    return pl.pallas_call(
        body,
        out_shape=vmem((LEAF, 2, 128), F32),
        in_specs=[hbm_spec] * 11,
        out_specs=pl.BlockSpec(memory_space=vmem),
        scratch_shapes=[
            vmem((LEAF, 2, 128), F32),
            vmem((SMP, 2 * LEAF + 16, 128), jnp.int16),
            vmem((3, 2, LEAF, 128), BF16),
            vmem((LEAF, SLOTS, 2, 128, 128), BF16),
            vmem((SLOTS, LEAF), I32),
            vmem((2, 128, 256), F32),
            vmem((256, 128), F32),
            vmem((8, 128), F32),
            vmem((1, GROUP), I32),
            vmem((1, GROUP), I32),
            vmem((TABLE, 2, 128), F32),
            vmem((64, PAR), I32),
            vmem((2, 256, 128), F32),
            vmem((TABLE, 128), F32),
            vmem((TABLE, 128), F32),
            vmem((3, 2, PAR, 128), F32),
            vmem((3, 2 * PAR + 16, 128), jnp.int16),
            vmem((768, 256), BF16),
            vmem((768, 256), BF16),
            vmem((GROUP, 256), F32),
            vmem((PAR, 512), BF16),
            vmem((GROUP, 192), BF16),
            vmem((WORDS, PAR, 128), I32),
            vmem((SLOTS * 256, 128), BF16),
            vmem((128, 128), F32),
            vmem((PAR, 256), F32),
            vmem((SMP, LEAF, 256), F32),
            vmem((SMP, 2 * LEAF + 16, 128), jnp.int16),
            vmem((SMP - 1, 2 * LEAF + 16, 128), jnp.int16),
            dma((11,)),
            dma((CHUNKS,)),
            dma((2,)),
            dma((2,)),
            dma((SMP - 1,)),
            dma((SMP - 1,)),
            dma((2,)),
            dma((2,)),
            dma((SMP - 1,)),
            dma((SMP - 1,)),
            pltpu.SemaphoreType.REGULAR,
            pltpu.SemaphoreType.REGULAR,
        ],
        compiler_params=pltpu.CompilerParams(
            collective_id=0, has_side_effects=True, vmem_limit_bytes=60 * 1024 * 1024
        ),
        name="far_and_near",
    )(
        currents,
        near_blocks,
        near_src.T,
        radiation,
        interp,
        shift_phase,
        parent_map,
        octant,
        trans,
        far_src.T,
        receive,
    )


def solution(mesh):
    in_specs = (
        P(("clu", "smp"), None, None),
        P(("clu", "smp"), None, None, None, None),
        P(("clu", "smp"), None),
        P(),
        P(),
        P(),
        P("clu", None),
        P("clu", None),
        P(None, None, "smp"),
        P("clu", None),
        P("clu", None),
        P(),
    )
    out_specs = P(("clu", "smp"), None, None)
    return jax.shard_map(
        on_device, mesh=mesh, in_specs=in_specs, out_specs=out_specs, check_vma=False
    )
```

```python
import functools

import jax
import jax.numpy as jnp
from jax import lax
from jax.experimental import pallas as pl
from jax.experimental.pallas import tpu as pltpu
from jax.sharding import PartitionSpec as P

MESH = pl.DeviceIdType.MESH
F32 = jnp.float32
BF16 = jnp.bfloat16
I32 = jnp.int32
HIGHEST = lax.Precision.HIGHEST
NN = (((1,), (0,)), ((), ()))
NT = (((1,), (1,)), ((), ()))
TN = (((0,), (0,)), ((), ()))

CLU = 16
SMP = 8
LEAF = 32
GROUP = 256
PAR = 96
SLOTS = 6
KINDS = 316
TABLE = 384
BLOCKS = PAR // 8
WORDS = 9
CHUNK = 8
CHUNKS = LEAF // CHUNK
EARLY = 1
STEPS = 32000.0
ORDER = (4, 3, 5, 2, 6, 1, 7)


def iota(shape, axis):
    return lax.broadcasted_iota(I32, shape, axis)


def mm(left, right, dims=NN, precision=None):
    return lax.dot_general(left, right, dims, precision=precision, preferred_element_type=F32)


def halves(value):
    high = value.astype(BF16)
    return high, (value - high.astype(F32)).astype(BF16)


def stacked(value):
    high, low = halves(value)
    return jnp.concatenate([high, low, high], axis=0)


def split3(value):
    high, low = halves(value)
    return jnp.concatenate([high, high, low], axis=1)


def coded(value):
    top = jnp.maximum(jnp.max(jnp.abs(value), axis=0, keepdims=True), 1e-30)
    power = jnp.ceil(jnp.log2(top))
    whole = jnp.floor(value * (STEPS * jnp.exp2(-power)) + 0.5)
    return whole.astype(I32), power


def message(parts):
    pairs = [coded(part) for part in parts]
    tail = [jnp.broadcast_to(power, (8, 128)).astype(I32) for _, power in pairs]
    return jnp.concatenate([whole for whole, _ in pairs] + tail, axis=0).astype(jnp.int16)


def decoded(block, rows):
    value = block.astype(I32).astype(F32)
    scale = [
        jnp.exp2(value[2 * rows + 8 * c : 2 * rows + 8 * c + 1]) * (1.0 / STEPS) for c in range(2)
    ]
    return [value[c * rows : (c + 1) * rows] * scale[c] for c in range(2)]


def complex_square(real, imag):
    return jnp.concatenate(
        [jnp.concatenate([real, imag], axis=1), jnp.concatenate([-imag, real], axis=1)], axis=0
    )


def far_masks(source):
    bits = jnp.left_shift(jnp.ones_like(source), source & 7).astype(F32)
    octet = lax.shift_right_logical(source, jnp.full_like(source, 3))
    rows = iota((40, PAR), 0)
    table = jnp.zeros((40, PAR), F32)
    for f in range(64):
        table = table + jnp.where(octet[f : f + 1] == rows, bits[f : f + 1], 0.0)
    flip = ((iota((PAR, PAR), 0) ^ 7) == iota((PAR, PAR), 1)).astype(BF16)
    table = jnp.concatenate([table, jnp.zeros((88, PAR), F32)], axis=0)
    octets = mm(flip, table.astype(BF16), NT).astype(I32)
    octets = jnp.left_shift(octets, 8 * (iota((PAR, 128), 1) & 3))
    pairs = octets + pltpu.roll(octets, 127, axis=1)
    return pairs + pltpu.roll(pairs, 126, axis=1)


def body(
    cur,
    blocks,
    near_src,
    rad,
    itp,
    phase,
    pmap,
    octant,
    trans,
    far_src,
    rec,
    out,
    cur_v,
    cur_msg,
    near_cur,
    near_blk,
    ns_v,
    rad_v,
    itp_v,
    ph_v,
    pm_v,
    oc_v,
    tr_v,
    fs_v,
    rec_v,
    t_re,
    t_im,
    upper,
    up_msg,
    m_op,
    n_op,
    shift,
    to_parent,
    to_leaf,
    words,
    near_x,
    near_acc,
    incoming,
    part,
    part_msg,
    arrived,
    load_sem,
    blk_sem,
    near_send,
    near_recv,
    cur_send,
    cur_recv,
    up_send,
    up_recv,
    part_send,
    part_recv,
    up_greet,
    near_greet,
):
    clu = lax.axis_index("clu")
    me = lax.axis_index("smp")
    device = clu * SMP + me
    after = device + 1
    before = device + CLU * SMP - 1
    after_id = (lax.rem(after // SMP, CLU), lax.rem(after, SMP))
    before_id = (lax.rem(before // SMP, CLU), lax.rem(before, SMP))
    up_id = (lax.rem(clu + 1, CLU), me)
    down_id = (lax.rem(clu + CLU - 1, CLU), me)
    peers = {o: (clu, lax.rem(me + o, SMP)) for o in range(1, SMP)}
    has_after, has_before = device < CLU * SMP - 1, device > 0
    has_up, has_down = clu < CLU - 1, clu > 0

    barrier = pltpu.get_barrier_semaphore()

    def greet(where):
        pl.semaphore_signal(barrier, inc=1, device_id=where, device_id_type=MESH)

    defers = (lax.rem(clu, 4) == 0) & has_down
    late = (lax.rem(clu, 4) == 3) & has_up
    near_defers = defers & (me == 0)
    near_late = late & (me == SMP - 1)

    greeted = SMP - 1
    for to, from_, where in (
        (has_after & jnp.logical_not(near_late), has_after, after_id),
        (has_before, has_before & jnp.logical_not(near_defers), before_id),
        (has_up & jnp.logical_not(late), has_up, up_id),
        (has_down, has_down & jnp.logical_not(defers), down_id),
    ):
        pl.when(to)(functools.partial(greet, where))
        greeted = greeted + from_.astype(I32)
    for where in peers.values():
        greet(where)

    columns = pl.ds(pl.multiple_of(me * 128, 128), 128)
    loads = [
        (cur, cur_v),
        (itp.at[:, columns], itp_v),
        (phase.at[:, columns], ph_v),
        (rad, rad_v),
        (rec, rec_v),
        (pmap, pm_v),
        (octant, oc_v),
        (far_src, fs_v),
        (near_src, ns_v),
        (trans.at[pl.ds(KINDS - 192, 192)], tr_v.at[pl.ds(0, 192)]),
        (trans.at[pl.ds(0, 192)], tr_v.at[pl.ds(192, 192)]),
    ]
    copies = [
        pltpu.make_async_copy(source, target, load_sem.at[i])
        for i, (source, target) in enumerate(loads)
    ]
    for copy in copies:
        copy.start()
    blk_copies = [
        pltpu.make_async_copy(
            blocks.at[pl.ds(i * CHUNK, CHUNK)], near_blk.at[pl.ds(i * CHUNK, CHUNK)], blk_sem.at[i]
        )
        for i in range(CHUNKS)
    ]
    for copy in blk_copies:
        copy.start()

    copies[0].wait()
    own_cur = [cur_v[:, c, :] for c in range(2)]
    for c in range(2):
        near_cur[1, c] = own_cur[c].astype(BF16)
    cur_msg[me] = message(own_cur)

    def clear(near_slot, up_slot):
        if near_slot is not None:
            near_cur[near_slot] = jnp.zeros((2, LEAF, 128), BF16)
        if up_slot is not None:
            up_msg[up_slot] = jnp.zeros((2 * PAR + 16, 128), jnp.int16)

    pl.when(jnp.logical_not(has_before))(functools.partial(clear, 0, None))
    pl.when(jnp.logical_not(has_after))(functools.partial(clear, 2, None))
    pl.when(jnp.logical_not(has_down))(functools.partial(clear, None, 0))
    pl.when(jnp.logical_not(has_up))(functools.partial(clear, None, 2))
    pl.semaphore_wait(barrier, greeted)

    def called(there, semaphore, where):
        @pl.when(there)
        def call():
            pl.semaphore_signal(semaphore, inc=1, device_id=where, device_id_type=MESH)

    called(late, up_greet, up_id)
    called(near_late, near_greet, after_id)
    near_out = [
        pltpu.make_async_remote_copy(
            src_ref=near_cur.at[1],
            dst_ref=near_cur.at[slot],
            send_sem=near_send.at[i],
            recv_sem=near_recv.at[i],
            device_id=where,
            device_id_type=MESH,
        )
        for i, (slot, where) in enumerate(((0, after_id), (2, before_id)))
    ]
    cur_out = [
        pltpu.make_async_remote_copy(
            src_ref=cur_msg.at[me],
            dst_ref=cur_msg.at[me],
            send_sem=cur_send.at[o - 1],
            recv_sem=cur_recv.at[o - 1],
            device_id=peers[o],
            device_id_type=MESH,
        )
        for o in ORDER
    ]
    for copy in cur_out:
        copy.start()
    for copy, there in zip(near_out, (has_after, has_before & jnp.logical_not(near_defers))):
        pl.when(there)(copy.start)

    for copy in copies[1:9]:
        copy.wait()
    grid = itp_v[...]
    both = mm(split3(rad_v[...].reshape(256, 256)), stacked(grid))
    m_op[...] = stacked(complex_square(both[:128], both[128:]))
    both = mm(grid, jnp.concatenate([rec_v[0], rec_v[1]], axis=1), TN, HIGHEST)
    n_op[...] = stacked(complex_square(both[:, :128], both[:, 128:]))
    angles = ph_v[...]
    table = jnp.concatenate([jnp.cos(angles), jnp.sin(angles)], axis=1)
    position = (oc_v[...] == iota((8, GROUP), 0)).astype(F32)
    shift[...] = mm(position, table, TN, HIGHEST)
    owner = pm_v[...]
    member = (owner == iota((PAR, GROUP), 0)).astype(BF16)
    to_parent[...] = jnp.concatenate([member, member], axis=1)
    member = (owner == (iota((PAR, GROUP), 0) ^ 7)).astype(F32)
    to_leaf[...] = jnp.concatenate([member, member], axis=0).T.astype(BF16)
    masks = far_masks(fs_v[...] - (clu - 1) * PAR)
    for q in range(WORDS):
        words[q] = jnp.broadcast_to(masks[:, 4 * q : 4 * q + 1], (PAR, 128))
    copies[9].wait()
    copies[10].wait()
    t_re[...] = tr_v[:, 0, :]
    t_im[...] = tr_v[:, 1, :]

    lane_leaf = lax.rem(iota((128, 128), 1), LEAF)

    def near_chunk(i, carry):
        first = pl.multiple_of(i * CHUNK, CHUNK)
        pltpu.make_async_copy(
            blocks.at[pl.ds(first, CHUNK)], near_blk.at[pl.ds(first, CHUNK)], blk_sem.at[i]
        ).wait()
        lhs = jnp.concatenate(
            [
                near_blk[pl.ds(first, CHUNK), s, c].reshape(CHUNK * 128, 128)
                for s in range(SLOTS)
                for c in range(2)
            ],
            axis=1,
        )
        result = mm(lhs, near_x[...])
        total = near_acc[...]
        for r in range(CHUNK):
            total = jnp.where(lane_leaf == first + r, result[r * 128 : (r + 1) * 128], total)
        near_acc[...] = total
        return carry

    for copy in cur_out:
        copy.wait_recv()
    x = jnp.concatenate(
        [jnp.concatenate(decoded(cur_msg[i], LEAF), axis=1) for i in range(SMP)], axis=0
    )
    inter = mm(split3(x), m_op[...])
    cos, sin = shift[:, :128], shift[:, 128:]
    real, imag = inter[:, :128], inter[:, 128:]
    shifted = jnp.concatenate([real * cos - imag * sin, real * sin + imag * cos], axis=1)
    own = mm(to_parent[...], jnp.concatenate(halves(shifted), axis=0))
    own = [own[:, :128], own[:, 128:]]
    for c in range(2):
        upper[1, c] = own[c]
    up_msg[1] = message(own)
    up_out = [
        pltpu.make_async_remote_copy(
            src_ref=up_msg.at[1],
            dst_ref=up_msg.at[slot],
            send_sem=up_send.at[i],
            recv_sem=up_recv.at[i],
            device_id=where,
            device_id_type=MESH,
        )
        for i, (slot, where) in enumerate(((0, up_id), (2, down_id)))
    ]
    pl.when(has_up)(up_out[0].start)

    @pl.when(defers)
    def await_late():
        pl.semaphore_wait(up_greet, 1)

    pl.when(has_down)(up_out[1].start)

    @pl.when(near_defers)
    def await_near_late():
        pl.semaphore_wait(near_greet, 1)
        near_out[1].start()

    def translate(group):
        def octet_step(step, sums):
            sums = list(sums)
            start = pl.multiple_of(8 * step, 8)
            up_re = upper[group, 0, pl.ds(start, 8)]
            up_im = upper[group, 1, pl.ds(start, 8)]
            offset = jnp.full((8, 128), 8 * lax.rem(step, 4), I32)
            word = 3 * group + step // 4
            marks = [
                lax.shift_right_logical(words[word, 8 * b : 8 * b + 8], offset)
                for b in range(BLOCKS)
            ]
            for i in range(8):
                source_re = jnp.broadcast_to(up_re[i : i + 1], (8, 128))
                source_im = jnp.broadcast_to(up_im[i : i + 1], (8, 128))
                for b in range(BLOCKS):
                    at = PAR * group + start + (89 + i - 8 * b)
                    op_re = t_re[pl.ds(at, 8)]
                    op_im = t_im[pl.ds(at, 8)]
                    there = (marks[b] & (1 << i)) != 0
                    here_re = jnp.where(there, source_re, 0.0)
                    here_im = jnp.where(there, source_im, 0.0)
                    sums[2 * b] = sums[2 * b] + (op_re * here_re - op_im * here_im)
                    sums[2 * b + 1] = sums[2 * b + 1] + (op_re * here_im + op_im * here_re)
            return tuple(sums)

        sums = tuple(
            incoming[8 * b : 8 * b + 8, 128 * c : 128 * c + 128]
            for b in range(BLOCKS)
            for c in range(2)
        )
        def octet_pair(pair, sums):
            return octet_step(2 * pair + 1, octet_step(2 * pair, sums))

        sums = lax.fori_loop(0, BLOCKS // 2, octet_pair, sums)
        for b in range(BLOCKS):
            for c in range(2):
                incoming[8 * b : 8 * b + 8, 128 * c : 128 * c + 128] = sums[2 * b + c]

    part_out = [
        pltpu.make_async_remote_copy(
            src_ref=part_msg.at[lax.rem(me + o, SMP)],
            dst_ref=arrived.at[o - 1],
            send_sem=part_send.at[o - 1],
            recv_sem=part_recv.at[o - 1],
            device_id=peers[o],
            device_id_type=MESH,
        )
        for o in ORDER
    ]

    def spread():
        field = mm(to_leaf[...], jnp.concatenate(halves(incoming[...]), axis=0))
        cos, sin = shift[:, :128], shift[:, 128:]
        real, imag = field[:, :128], field[:, 128:]
        back = jnp.concatenate([real * cos + imag * sin, imag * cos - real * sin], axis=1)
        result = mm(split3(back), n_op[...])
        part[...] = result.reshape(SMP, LEAF, 256)
        for i in range(SMP):
            rows = result[i * LEAF : (i + 1) * LEAF]
            part_msg[i] = message([rows[:, :128], rows[:, 128:]])
        for copy in part_out:
            copy.start()

    incoming[...] = jnp.zeros((PAR, 256), F32)
    near_acc[...] = jnp.zeros((128, 128), F32)

    def near_sides():
        for copy, there in zip(near_out, (has_before, has_after)):
            pl.when(there)(copy.wait_recv)
        p_re = near_cur[:, 0].reshape(PAR, 128).astype(F32)
        p_im = near_cur[:, 1].reshape(PAR, 128).astype(F32)
        sources = jnp.concatenate(
            [jnp.concatenate([p_re, -p_im], axis=1), jnp.concatenate([p_im, p_re], axis=1)], axis=0
        )
        local = ns_v[...] - (device - 1) * LEAF
        local = jnp.concatenate(
            [local, local + PAR, jnp.full((SLOTS, 64), -1, I32)], axis=1
        )
        rows = iota((2 * PAR, 128), 0)
        picks = jnp.concatenate(
            [(local[s : s + 1] == rows).astype(F32) for s in range(SLOTS)], axis=1
        ).astype(BF16)
        rhs = mm(sources.T.astype(BF16), picks).astype(BF16)
        for s in range(SLOTS):
            near_x[pl.ds(s * 256, 256)] = rhs[:, s * 128 : (s + 1) * 128]

    order = jnp.where(lax.rem(clu, 4) == 0, 1, 2)

    ahead = jnp.where(lax.rem(clu, 4) == 0, EARLY, 0)
    sides_at = jnp.where(lax.rem(clu, 4) == 0, 0, 2)

    def phase(turn, carry):
        group = lax.rem(1 + order * turn, 3)
        pl.when((group == 0) & has_down)(up_out[0].wait_recv)
        pl.when((group == 2) & has_up)(up_out[1].wait_recv)
        missing = ((group == 0) & jnp.logical_not(has_down)) | (
            (group == 2) & jnp.logical_not(has_up)
        )

        @pl.when(turn > 0)
        def take():
            for c, value in enumerate(decoded(up_msg[group], PAR)):
                upper[group, c] = value

        pl.when(jnp.logical_not(missing))(functools.partial(translate, group))
        pl.when(turn == 2)(spread)
        pl.when(turn == sides_at)(near_sides)
        lax.fori_loop(
            jnp.where(turn == 0, 0, ahead),
            jnp.where(turn == 2, CHUNKS, ahead),
            near_chunk,
            0,
        )
        return carry

    lax.fori_loop(0, 3, phase, 0)

    near = near_acc[...].T
    total = part[me] + jnp.concatenate([near[:LEAF], near[LEAF : 2 * LEAF]], axis=1)
    for copy, o in zip(part_out, ORDER):
        copy.wait_recv()
        total = total + jnp.concatenate(decoded(arrived[o - 1], LEAF), axis=1)
    out[:, 0, :] = total[:, :128]
    out[:, 1, :] = total[:, 128:]
    for copy, there in zip((*near_out, *up_out), (has_after, has_before, has_up, has_down)):
        pl.when(there)(copy.wait_send)
    for copy in (*cur_out, *part_out):
        copy.wait_send()


def on_device(
    currents,
    near_blocks,
    near_src,
    radiation,
    interp,
    shift_phase,
    parent_map,
    octant,
    trans,
    far_src,
    far_kind,
    receive,
):
    hbm_spec = pl.BlockSpec(memory_space=pltpu.HBM)
    vmem = pltpu.VMEM
    dma = pltpu.SemaphoreType.DMA
    return pl.pallas_call(
        body,
        out_shape=vmem((LEAF, 2, 128), F32),
        in_specs=[hbm_spec] * 11,
        out_specs=pl.BlockSpec(memory_space=vmem),
        scratch_shapes=[
            vmem((LEAF, 2, 128), F32),
            vmem((SMP, 2 * LEAF + 16, 128), jnp.int16),
            vmem((3, 2, LEAF, 128), BF16),
            vmem((LEAF, SLOTS, 2, 128, 128), BF16),
            vmem((SLOTS, LEAF), I32),
            vmem((2, 128, 256), F32),
            vmem((256, 128), F32),
            vmem((8, 128), F32),
            vmem((1, GROUP), I32),
            vmem((1, GROUP), I32),
            vmem((TABLE, 2, 128), F32),
            vmem((64, PAR), I32),
            vmem((2, 256, 128), F32),
            vmem((TABLE, 128), F32),
            vmem((TABLE, 128), F32),
            vmem((3, 2, PAR, 128), F32),
            vmem((3, 2 * PAR + 16, 128), jnp.int16),
            vmem((768, 256), BF16),
            vmem((768, 256), BF16),
            vmem((GROUP, 256), F32),
            vmem((PAR, 512), BF16),
            vmem((GROUP, 192), BF16),
            vmem((WORDS, PAR, 128), I32),
            vmem((SLOTS * 256, 128), BF16),
            vmem((128, 128), F32),
            vmem((PAR, 256), F32),
            vmem((SMP, LEAF, 256), F32),
            vmem((SMP, 2 * LEAF + 16, 128), jnp.int16),
            vmem((SMP - 1, 2 * LEAF + 16, 128), jnp.int16),
            dma((11,)),
            dma((CHUNKS,)),
            dma((2,)),
            dma((2,)),
            dma((SMP - 1,)),
            dma((SMP - 1,)),
            dma((2,)),
            dma((2,)),
            dma((SMP - 1,)),
            dma((SMP - 1,)),
            pltpu.SemaphoreType.REGULAR,
            pltpu.SemaphoreType.REGULAR,
        ],
        compiler_params=pltpu.CompilerParams(
            collective_id=0, has_side_effects=True, vmem_limit_bytes=60 * 1024 * 1024
        ),
        name="far_and_near",
    )(
        currents,
        near_blocks,
        near_src.T,
        radiation,
        interp,
        shift_phase,
        parent_map,
        octant,
        trans,
        far_src.T,
        receive,
    )


def solution(mesh):
    in_specs = (
        P(("clu", "smp"), None, None),
        P(("clu", "smp"), None, None, None, None),
        P(("clu", "smp"), None),
        P(),
        P(),
        P(),
        P("clu", None),
        P("clu", None),
        P(None, None, "smp"),
        P("clu", None),
        P("clu", None),
        P(),
    )
    out_specs = P(("clu", "smp"), None, None)
    return jax.shard_map(
        on_device, mesh=mesh, in_specs=in_specs, out_specs=out_specs, check_vma=False
    )
```

```python
import functools

import jax
import jax.numpy as jnp
from jax import lax
from jax.experimental import pallas as pl
from jax.experimental.pallas import tpu as pltpu
from jax.sharding import PartitionSpec as P

MESH = pl.DeviceIdType.MESH
F32 = jnp.float32
BF16 = jnp.bfloat16
I32 = jnp.int32
HIGHEST = lax.Precision.HIGHEST
NN = (((1,), (0,)), ((), ()))
NT = (((1,), (1,)), ((), ()))
TN = (((0,), (0,)), ((), ()))

CLU = 16
SMP = 8
LEAF = 32
GROUP = 256
PAR = 96
SLOTS = 6
KINDS = 316
TABLE = 384
BLOCKS = PAR // 8
WORDS = 9
CHUNK = 8
CHUNKS = LEAF // CHUNK
EARLY = 1
STEPS = 32000.0
ORDER = (4, 3, 5, 2, 6, 1, 7)


def iota(shape, axis):
    return lax.broadcasted_iota(I32, shape, axis)


def mm(left, right, dims=NN, precision=None):
    return lax.dot_general(left, right, dims, precision=precision, preferred_element_type=F32)


def halves(value):
    high = value.astype(BF16)
    return high, (value - high.astype(F32)).astype(BF16)


def stacked(value):
    high, low = halves(value)
    return jnp.concatenate([high, low, high], axis=0)


def split3(value):
    high, low = halves(value)
    return jnp.concatenate([high, high, low], axis=1)


def coded(value):
    top = jnp.maximum(jnp.max(jnp.abs(value), axis=0, keepdims=True), 1e-30)
    power = jnp.ceil(jnp.log2(top))
    whole = jnp.floor(value * (STEPS * jnp.exp2(-power)) + 0.5)
    return whole.astype(I32), power


def message(parts):
    pairs = [coded(part) for part in parts]
    tail = [jnp.broadcast_to(power, (8, 128)).astype(I32) for _, power in pairs]
    return jnp.concatenate([whole for whole, _ in pairs] + tail, axis=0).astype(jnp.int16)


def decoded(block, rows):
    value = block.astype(I32).astype(F32)
    scale = [
        jnp.exp2(value[2 * rows + 8 * c : 2 * rows + 8 * c + 1]) * (1.0 / STEPS) for c in range(2)
    ]
    return [value[c * rows : (c + 1) * rows] * scale[c] for c in range(2)]


def complex_square(real, imag):
    return jnp.concatenate(
        [jnp.concatenate([real, imag], axis=1), jnp.concatenate([-imag, real], axis=1)], axis=0
    )


def far_masks(source):
    bits = jnp.left_shift(jnp.ones_like(source), source & 7).astype(F32)
    octet = lax.shift_right_logical(source, jnp.full_like(source, 3))
    rows = iota((40, PAR), 0)
    table = jnp.zeros((40, PAR), F32)
    for f in range(64):
        table = table + jnp.where(octet[f : f + 1] == rows, bits[f : f + 1], 0.0)
    flip = ((iota((PAR, PAR), 0) ^ 7) == iota((PAR, PAR), 1)).astype(BF16)
    table = jnp.concatenate([table, jnp.zeros((88, PAR), F32)], axis=0)
    octets = mm(flip, table.astype(BF16), NT).astype(I32)
    octets = jnp.left_shift(octets, 8 * (iota((PAR, 128), 1) & 3))
    pairs = octets + pltpu.roll(octets, 127, axis=1)
    return pairs + pltpu.roll(pairs, 126, axis=1)


def body(
    cur,
    blocks,
    near_src,
    rad,
    itp,
    phase,
    pmap,
    octant,
    trans,
    far_src,
    rec,
    out,
    cur_v,
    cur_msg,
    near_cur,
    near_blk,
    ns_v,
    rad_v,
    itp_v,
    ph_v,
    pm_v,
    oc_v,
    tr_v,
    fs_v,
    rec_v,
    t_re,
    t_minus,
    t_plus,
    upper,
    up_msg,
    m_op,
    n_op,
    shift,
    to_parent,
    to_leaf,
    words,
    near_x,
    near_acc,
    incoming,
    part,
    part_msg,
    arrived,
    load_sem,
    blk_sem,
    near_send,
    near_recv,
    cur_send,
    cur_recv,
    up_send,
    up_recv,
    part_send,
    part_recv,
    up_greet,
    near_greet,
):
    clu = lax.axis_index("clu")
    me = lax.axis_index("smp")
    device = clu * SMP + me
    after = device + 1
    before = device + CLU * SMP - 1
    after_id = (lax.rem(after // SMP, CLU), lax.rem(after, SMP))
    before_id = (lax.rem(before // SMP, CLU), lax.rem(before, SMP))
    up_id = (lax.rem(clu + 1, CLU), me)
    down_id = (lax.rem(clu + CLU - 1, CLU), me)
    peers = {o: (clu, lax.rem(me + o, SMP)) for o in range(1, SMP)}
    has_after, has_before = device < CLU * SMP - 1, device > 0
    has_up, has_down = clu < CLU - 1, clu > 0

    barrier = pltpu.get_barrier_semaphore()

    def greet(where):
        pl.semaphore_signal(barrier, inc=1, device_id=where, device_id_type=MESH)

    defers = (lax.rem(clu, 4) == 0) & has_down
    late = (lax.rem(clu, 4) == 3) & has_up
    near_defers = defers & (me == 0)
    near_late = late & (me == SMP - 1)

    greeted = SMP - 1
    for to, from_, where in (
        (has_after & jnp.logical_not(near_late), has_after, after_id),
        (has_before, has_before & jnp.logical_not(near_defers), before_id),
        (has_up & jnp.logical_not(late), has_up, up_id),
        (has_down, has_down & jnp.logical_not(defers), down_id),
    ):
        pl.when(to)(functools.partial(greet, where))
        greeted = greeted + from_.astype(I32)
    for where in peers.values():
        greet(where)

    columns = pl.ds(pl.multiple_of(me * 128, 128), 128)
    loads = [
        (cur, cur_v),
        (itp.at[:, columns], itp_v),
        (phase.at[:, columns], ph_v),
        (rad, rad_v),
        (rec, rec_v),
        (pmap, pm_v),
        (octant, oc_v),
        (far_src, fs_v),
        (near_src, ns_v),
        (trans.at[pl.ds(KINDS - 192, 192)], tr_v.at[pl.ds(0, 192)]),
        (trans.at[pl.ds(0, 192)], tr_v.at[pl.ds(192, 192)]),
    ]
    copies = [
        pltpu.make_async_copy(source, target, load_sem.at[i])
        for i, (source, target) in enumerate(loads)
    ]
    for copy in copies:
        copy.start()
    blk_copies = [
        pltpu.make_async_copy(
            blocks.at[pl.ds(i * CHUNK, CHUNK)], near_blk.at[pl.ds(i * CHUNK, CHUNK)], blk_sem.at[i]
        )
        for i in range(CHUNKS)
    ]
    for copy in blk_copies:
        copy.start()

    copies[0].wait()
    own_cur = [cur_v[:, c, :] for c in range(2)]
    for c in range(2):
        near_cur[1, c] = own_cur[c].astype(BF16)
    cur_msg[me] = message(own_cur)

    def clear(near_slot, up_slot):
        if near_slot is not None:
            near_cur[near_slot] = jnp.zeros((2, LEAF, 128), BF16)
        if up_slot is not None:
            up_msg[up_slot] = jnp.zeros((2 * PAR + 16, 128), jnp.int16)

    pl.when(jnp.logical_not(has_before))(functools.partial(clear, 0, None))
    pl.when(jnp.logical_not(has_after))(functools.partial(clear, 2, None))
    pl.when(jnp.logical_not(has_down))(functools.partial(clear, None, 0))
    pl.when(jnp.logical_not(has_up))(functools.partial(clear, None, 2))
    pl.semaphore_wait(barrier, greeted)

    def called(there, semaphore, where):
        @pl.when(there)
        def call():
            pl.semaphore_signal(semaphore, inc=1, device_id=where, device_id_type=MESH)

    called(late, up_greet, up_id)
    called(near_late, near_greet, after_id)
    near_out = [
        pltpu.make_async_remote_copy(
            src_ref=near_cur.at[1],
            dst_ref=near_cur.at[slot],
            send_sem=near_send.at[i],
            recv_sem=near_recv.at[i],
            device_id=where,
            device_id_type=MESH,
        )
        for i, (slot, where) in enumerate(((0, after_id), (2, before_id)))
    ]
    cur_out = [
        pltpu.make_async_remote_copy(
            src_ref=cur_msg.at[me],
            dst_ref=cur_msg.at[me],
            send_sem=cur_send.at[o - 1],
            recv_sem=cur_recv.at[o - 1],
            device_id=peers[o],
            device_id_type=MESH,
        )
        for o in ORDER
    ]
    for copy in cur_out:
        copy.start()
    across = (has_after & (me == SMP - 1), has_before & (me == 0) & jnp.logical_not(near_defers))
    for copy, there in zip(near_out, across):
        pl.when(there)(copy.start)

    for copy in copies[1:9]:
        copy.wait()
    grid = itp_v[...]
    both = mm(split3(rad_v[...].reshape(256, 256)), stacked(grid))
    m_op[...] = stacked(complex_square(both[:128], both[128:]))
    both = mm(grid, jnp.concatenate([rec_v[0], rec_v[1]], axis=1), TN, HIGHEST)
    n_op[...] = stacked(complex_square(both[:, :128], both[:, 128:]))
    angles = ph_v[...]
    table = jnp.concatenate([jnp.cos(angles), jnp.sin(angles)], axis=1)
    position = (oc_v[...] == iota((8, GROUP), 0)).astype(F32)
    shift[...] = mm(position, table, TN, HIGHEST)
    owner = pm_v[...]
    member = (owner == iota((PAR, GROUP), 0)).astype(BF16)
    to_parent[...] = jnp.concatenate([member, member], axis=1)
    member = (owner == (iota((PAR, GROUP), 0) ^ 7)).astype(F32)
    to_leaf[...] = jnp.concatenate([member, member], axis=0).T.astype(BF16)
    masks = far_masks(fs_v[...] - (clu - 1) * PAR)
    for q in range(WORDS):
        words[q] = jnp.broadcast_to(masks[:, 4 * q : 4 * q + 1], (PAR, 128))
    copies[9].wait()
    copies[10].wait()
    t_re[...] = tr_v[:, 0, :]
    t_minus[...] = tr_v[:, 1, :] - tr_v[:, 0, :]
    t_plus[...] = tr_v[:, 1, :] + tr_v[:, 0, :]

    lane_leaf = lax.rem(iota((128, 128), 1), LEAF)

    def near_chunk(i, carry):
        first = pl.multiple_of(i * CHUNK, CHUNK)
        pltpu.make_async_copy(
            blocks.at[pl.ds(first, CHUNK)], near_blk.at[pl.ds(first, CHUNK)], blk_sem.at[i]
        ).wait()
        lhs = jnp.concatenate(
            [
                near_blk[pl.ds(first, CHUNK), s, c].reshape(CHUNK * 128, 128)
                for s in range(SLOTS)
                for c in range(2)
            ],
            axis=1,
        )
        result = mm(lhs, near_x[...])
        total = near_acc[...]
        for r in range(CHUNK):
            total = jnp.where(lane_leaf == first + r, result[r * 128 : (r + 1) * 128], total)
        near_acc[...] = total
        return carry

    for copy in cur_out:
        copy.wait_recv()
    x = jnp.concatenate(
        [jnp.concatenate(decoded(cur_msg[i], LEAF), axis=1) for i in range(SMP)], axis=0
    )
    inter = mm(split3(x), m_op[...])
    cos, sin = shift[:, :128], shift[:, 128:]
    real, imag = inter[:, :128], inter[:, 128:]
    shifted = jnp.concatenate([real * cos - imag * sin, real * sin + imag * cos], axis=1)
    own = mm(to_parent[...], jnp.concatenate(halves(shifted), axis=0))
    own = [own[:, :128], own[:, 128:]]
    for c in range(2):
        upper[1, c] = own[c]
    up_msg[1] = message(own)
    up_out = [
        pltpu.make_async_remote_copy(
            src_ref=up_msg.at[1],
            dst_ref=up_msg.at[slot],
            send_sem=up_send.at[i],
            recv_sem=up_recv.at[i],
            device_id=where,
            device_id_type=MESH,
        )
        for i, (slot, where) in enumerate(((0, up_id), (2, down_id)))
    ]
    pl.when(has_up)(up_out[0].start)

    @pl.when(defers)
    def await_late():
        pl.semaphore_wait(up_greet, 1)

    pl.when(has_down)(up_out[1].start)

    for copy, there in zip(near_out, (me < SMP - 1, me > 0)):
        pl.when(there)(copy.start)

    @pl.when(near_defers)
    def await_near_late():
        pl.semaphore_wait(near_greet, 1)
        near_out[1].start()

    def translate(group):
        def octet_step(step, sums):
            sums = list(sums)
            start = pl.multiple_of(8 * step, 8)
            up_re = upper[group, 0, pl.ds(start, 8)]
            up_im = upper[group, 1, pl.ds(start, 8)]
            offset = jnp.full((8, 128), 8 * lax.rem(step, 4), I32)
            word = 3 * group + step // 4
            marks = [
                lax.shift_right_logical(words[word, 8 * b : 8 * b + 8], offset)
                for b in range(BLOCKS)
            ]
            for i in range(8):
                source_re = jnp.broadcast_to(up_re[i : i + 1], (8, 128))
                source_im = jnp.broadcast_to(up_im[i : i + 1], (8, 128))
                source_sum = source_re + source_im
                for b in range(BLOCKS):
                    at = PAR * group + start + (89 + i - 8 * b)
                    op_re = t_re[pl.ds(at, 8)]
                    op_minus = t_minus[pl.ds(at, 8)]
                    op_plus = t_plus[pl.ds(at, 8)]
                    there = (marks[b] & (1 << i)) != 0
                    here_re = jnp.where(there, source_re, 0.0)
                    here_im = jnp.where(there, source_im, 0.0)
                    here_sum = jnp.where(there, source_sum, 0.0)
                    sums[3 * b] = sums[3 * b] + op_re * here_sum
                    sums[3 * b + 1] = sums[3 * b + 1] + op_minus * here_re
                    sums[3 * b + 2] = sums[3 * b + 2] + op_plus * here_im
            return tuple(sums)

        sums = tuple(jnp.zeros((8, 128), F32) for _ in range(3 * BLOCKS))
        def octet_pair(pair, sums):
            return octet_step(2 * pair + 1, octet_step(2 * pair, sums))

        sums = lax.fori_loop(0, BLOCKS // 2, octet_pair, sums)
        for b in range(BLOCKS):
            both, minus, plus = sums[3 * b : 3 * b + 3]
            for c, value in enumerate((both - plus, both + minus)):
                place = (pl.ds(8 * b, 8), pl.ds(128 * c, 128))
                incoming[place] = incoming[place] + value

    part_out = [
        pltpu.make_async_remote_copy(
            src_ref=part_msg.at[lax.rem(me + o, SMP)],
            dst_ref=arrived.at[o - 1],
            send_sem=part_send.at[o - 1],
            recv_sem=part_recv.at[o - 1],
            device_id=peers[o],
            device_id_type=MESH,
        )
        for o in ORDER
    ]

    def spread():
        field = mm(to_leaf[...], jnp.concatenate(halves(incoming[...]), axis=0))
        cos, sin = shift[:, :128], shift[:, 128:]
        real, imag = field[:, :128], field[:, 128:]
        back = jnp.concatenate([real * cos + imag * sin, imag * cos - real * sin], axis=1)
        result = mm(split3(back), n_op[...])
        part[...] = result.reshape(SMP, LEAF, 256)
        for i in range(SMP):
            rows = result[i * LEAF : (i + 1) * LEAF]
            part_msg[i] = message([rows[:, :128], rows[:, 128:]])
        for copy in part_out:
            copy.start()

    incoming[...] = jnp.zeros((PAR, 256), F32)
    near_acc[...] = jnp.zeros((128, 128), F32)

    def near_sides():
        for copy, there in zip(near_out, (has_before, has_after)):
            pl.when(there)(copy.wait_recv)
        p_re = near_cur[:, 0].reshape(PAR, 128).astype(F32)
        p_im = near_cur[:, 1].reshape(PAR, 128).astype(F32)
        sources = jnp.concatenate(
            [jnp.concatenate([p_re, -p_im], axis=1), jnp.concatenate([p_im, p_re], axis=1)], axis=0
        )
        local = ns_v[...] - (device - 1) * LEAF
        local = jnp.concatenate(
            [local, local + PAR, jnp.full((SLOTS, 64), -1, I32)], axis=1
        )
        rows = iota((2 * PAR, 128), 0)
        picks = jnp.concatenate(
            [(local[s : s + 1] == rows).astype(F32) for s in range(SLOTS)], axis=1
        ).astype(BF16)
        rhs = mm(sources.T.astype(BF16), picks).astype(BF16)
        for s in range(SLOTS):
            near_x[pl.ds(s * 256, 256)] = rhs[:, s * 128 : (s + 1) * 128]

    order = jnp.where(lax.rem(clu, 4) == 0, 1, 2)

    ahead = jnp.where(lax.rem(clu, 4) == 0, EARLY, 0)
    sides_at = jnp.where(lax.rem(clu, 4) == 0, 0, 2)

    def phase(turn, carry):
        group = lax.rem(1 + order * turn, 3)
        pl.when((group == 0) & has_down)(up_out[0].wait_recv)
        pl.when((group == 2) & has_up)(up_out[1].wait_recv)
        missing = ((group == 0) & jnp.logical_not(has_down)) | (
            (group == 2) & jnp.logical_not(has_up)
        )

        @pl.when(turn > 0)
        def take():
            for c, value in enumerate(decoded(up_msg[group], PAR)):
                upper[group, c] = value

        pl.when(jnp.logical_not(missing))(functools.partial(translate, group))
        pl.when(turn == 2)(spread)
        pl.when(turn == sides_at)(near_sides)
        lax.fori_loop(
            jnp.where(turn == 0, 0, ahead),
            jnp.where(turn == 2, CHUNKS, ahead),
            near_chunk,
            0,
        )
        return carry

    lax.fori_loop(0, 3, phase, 0)

    near = near_acc[...].T
    total = part[me] + jnp.concatenate([near[:LEAF], near[LEAF : 2 * LEAF]], axis=1)
    for copy, o in zip(part_out, ORDER):
        copy.wait_recv()
        total = total + jnp.concatenate(decoded(arrived[o - 1], LEAF), axis=1)
    out[:, 0, :] = total[:, :128]
    out[:, 1, :] = total[:, 128:]
    for copy, there in zip((*near_out, *up_out), (has_after, has_before, has_up, has_down)):
        pl.when(there)(copy.wait_send)
    for copy in (*cur_out, *part_out):
        copy.wait_send()


def on_device(
    currents,
    near_blocks,
    near_src,
    radiation,
    interp,
    shift_phase,
    parent_map,
    octant,
    trans,
    far_src,
    far_kind,
    receive,
):
    hbm_spec = pl.BlockSpec(memory_space=pltpu.HBM)
    vmem = pltpu.VMEM
    dma = pltpu.SemaphoreType.DMA
    return pl.pallas_call(
        body,
        out_shape=vmem((LEAF, 2, 128), F32),
        in_specs=[hbm_spec] * 11,
        out_specs=pl.BlockSpec(memory_space=vmem),
        scratch_shapes=[
            vmem((LEAF, 2, 128), F32),
            vmem((SMP, 2 * LEAF + 16, 128), jnp.int16),
            vmem((3, 2, LEAF, 128), BF16),
            vmem((LEAF, SLOTS, 2, 128, 128), BF16),
            vmem((SLOTS, LEAF), I32),
            vmem((2, 128, 256), F32),
            vmem((256, 128), F32),
            vmem((8, 128), F32),
            vmem((1, GROUP), I32),
            vmem((1, GROUP), I32),
            vmem((TABLE, 2, 128), F32),
            vmem((64, PAR), I32),
            vmem((2, 256, 128), F32),
            vmem((TABLE, 128), F32),
            vmem((TABLE, 128), F32),
            vmem((TABLE, 128), F32),
            vmem((3, 2, PAR, 128), F32),
            vmem((3, 2 * PAR + 16, 128), jnp.int16),
            vmem((768, 256), BF16),
            vmem((768, 256), BF16),
            vmem((GROUP, 256), F32),
            vmem((PAR, 512), BF16),
            vmem((GROUP, 192), BF16),
            vmem((WORDS, PAR, 128), I32),
            vmem((SLOTS * 256, 128), BF16),
            vmem((128, 128), F32),
            vmem((PAR, 256), F32),
            vmem((SMP, LEAF, 256), F32),
            vmem((SMP, 2 * LEAF + 16, 128), jnp.int16),
            vmem((SMP - 1, 2 * LEAF + 16, 128), jnp.int16),
            dma((11,)),
            dma((CHUNKS,)),
            dma((2,)),
            dma((2,)),
            dma((SMP - 1,)),
            dma((SMP - 1,)),
            dma((2,)),
            dma((2,)),
            dma((SMP - 1,)),
            dma((SMP - 1,)),
            pltpu.SemaphoreType.REGULAR,
            pltpu.SemaphoreType.REGULAR,
        ],
        compiler_params=pltpu.CompilerParams(
            collective_id=0, has_side_effects=True, vmem_limit_bytes=60 * 1024 * 1024
        ),
        name="far_and_near",
    )(
        currents,
        near_blocks,
        near_src.T,
        radiation,
        interp,
        shift_phase,
        parent_map,
        octant,
        trans,
        far_src.T,
        receive,
    )


def solution(mesh):
    in_specs = (
        P(("clu", "smp"), None, None),
        P(("clu", "smp"), None, None, None, None),
        P(("clu", "smp"), None),
        P(),
        P(),
        P(),
        P("clu", None),
        P("clu", None),
        P(None, None, "smp"),
        P("clu", None),
        P("clu", None),
        P(),
    )
    out_specs = P(("clu", "smp"), None, None)
    return jax.shard_map(
        on_device, mesh=mesh, in_specs=in_specs, out_specs=out_specs, check_vma=False
    )
```

```python
import functools

import jax
import jax.numpy as jnp
from jax import lax
from jax.experimental import pallas as pl
from jax.experimental.pallas import tpu as pltpu
from jax.sharding import PartitionSpec as P

MESH = pl.DeviceIdType.MESH
F32 = jnp.float32
BF16 = jnp.bfloat16
I32 = jnp.int32
HIGHEST = lax.Precision.HIGHEST
NN = (((1,), (0,)), ((), ()))
NT = (((1,), (1,)), ((), ()))
TN = (((0,), (0,)), ((), ()))

CLU = 16
SMP = 8
LEAF = 32
GROUP = 256
PAR = 96
SLOTS = 6
KINDS = 316
TABLE = 384
BLOCKS = PAR // 8
WORDS = 9
CHUNK = 8
CHUNKS = LEAF // CHUNK
EARLY = 1
STEPS = 32000.0
ORDER = (4, 3, 5, 2, 6, 1, 7)


def iota(shape, axis):
    return lax.broadcasted_iota(I32, shape, axis)


def mm(left, right, dims=NN, precision=None):
    return lax.dot_general(left, right, dims, precision=precision, preferred_element_type=F32)


def halves(value):
    high = value.astype(BF16)
    return high, (value - high.astype(F32)).astype(BF16)


def stacked(value):
    high, low = halves(value)
    return jnp.concatenate([high, low, high], axis=0)


def split3(value):
    high, low = halves(value)
    return jnp.concatenate([high, high, low], axis=1)


def coded(value):
    top = jnp.maximum(jnp.max(jnp.abs(value), axis=0, keepdims=True), 1e-30)
    power = jnp.ceil(jnp.log2(top))
    whole = jnp.floor(value * (STEPS * jnp.exp2(-power)) + 0.5)
    return whole.astype(I32), power


def message(parts):
    pairs = [coded(part) for part in parts]
    tail = [jnp.broadcast_to(power, (8, 128)).astype(I32) for _, power in pairs]
    return jnp.concatenate([whole for whole, _ in pairs] + tail, axis=0).astype(jnp.int16)


def decoded(block, rows):
    value = block.astype(I32).astype(F32)
    scale = [
        jnp.exp2(value[2 * rows + 8 * c : 2 * rows + 8 * c + 1]) * (1.0 / STEPS) for c in range(2)
    ]
    return [value[c * rows : (c + 1) * rows] * scale[c] for c in range(2)]


def complex_square(real, imag):
    return jnp.concatenate(
        [jnp.concatenate([real, imag], axis=1), jnp.concatenate([-imag, real], axis=1)], axis=0
    )


def far_masks(source):
    bits = jnp.left_shift(jnp.ones_like(source), source & 7).astype(F32)
    octet = lax.shift_right_logical(source, jnp.full_like(source, 3))
    rows = iota((40, PAR), 0)
    table = jnp.zeros((40, PAR), F32)
    for f in range(64):
        table = table + jnp.where(octet[f : f + 1] == rows, bits[f : f + 1], 0.0)
    flip = ((iota((PAR, PAR), 0) ^ 7) == iota((PAR, PAR), 1)).astype(BF16)
    table = jnp.concatenate([table, jnp.zeros((88, PAR), F32)], axis=0)
    octets = mm(flip, table.astype(BF16), NT).astype(I32)
    octets = jnp.left_shift(octets, 8 * (iota((PAR, 128), 1) & 3))
    pairs = octets + pltpu.roll(octets, 127, axis=1)
    return pairs + pltpu.roll(pairs, 126, axis=1)


def body(
    cur,
    blocks,
    near_src,
    rad,
    itp,
    phase,
    pmap,
    octant,
    trans,
    far_src,
    rec,
    out,
    cur_v,
    cur_msg,
    near_cur,
    near_blk,
    ns_v,
    rad_v,
    itp_v,
    ph_v,
    pm_v,
    oc_v,
    tr_v,
    fs_v,
    rec_v,
    t_re,
    t_minus,
    t_plus,
    upper,
    up_msg,
    m_op,
    n_op,
    shift,
    to_parent,
    to_leaf,
    words,
    near_x,
    near_acc,
    incoming,
    part,
    part_msg,
    arrived,
    load_sem,
    blk_sem,
    near_send,
    near_recv,
    cur_send,
    cur_recv,
    up_send,
    up_recv,
    part_send,
    part_recv,
    up_greet,
    near_greet,
):
    clu = lax.axis_index("clu")
    me = lax.axis_index("smp")
    device = clu * SMP + me
    after = device + 1
    before = device + CLU * SMP - 1
    after_id = (lax.rem(after // SMP, CLU), lax.rem(after, SMP))
    before_id = (lax.rem(before // SMP, CLU), lax.rem(before, SMP))
    up_id = (lax.rem(clu + 1, CLU), me)
    down_id = (lax.rem(clu + CLU - 1, CLU), me)
    peers = {o: (clu, lax.rem(me + o, SMP)) for o in range(1, SMP)}
    has_after, has_before = device < CLU * SMP - 1, device > 0
    has_up, has_down = clu < CLU - 1, clu > 0

    load_cur = pltpu.make_async_copy(cur, cur_v, load_sem.at[0])
    load_cur.start()
    barrier = pltpu.get_barrier_semaphore()

    def greet(where):
        pl.semaphore_signal(barrier, inc=1, device_id=where, device_id_type=MESH)

    defers = (lax.rem(clu, 4) == 0) & has_down
    late = (lax.rem(clu, 4) == 3) & has_up
    near_defers = defers & (me == 0)
    near_late = late & (me == SMP - 1)

    greeted = SMP - 1
    for to, from_, where in (
        (has_after & jnp.logical_not(near_late), has_after, after_id),
        (has_before, has_before & jnp.logical_not(near_defers), before_id),
        (has_up & jnp.logical_not(late), has_up, up_id),
        (has_down, has_down & jnp.logical_not(defers), down_id),
    ):
        pl.when(to)(functools.partial(greet, where))
        greeted = greeted + from_.astype(I32)
    for where in peers.values():
        greet(where)

    columns = pl.ds(pl.multiple_of(me * 128, 128), 128)
    loads = [
        (itp.at[:, columns], itp_v),
        (phase.at[:, columns], ph_v),
        (rad, rad_v),
        (rec, rec_v),
        (pmap, pm_v),
        (octant, oc_v),
        (far_src, fs_v),
        (near_src, ns_v),
        (trans.at[pl.ds(KINDS - 192, 192)], tr_v.at[pl.ds(0, 192)]),
        (trans.at[pl.ds(0, 192)], tr_v.at[pl.ds(192, 192)]),
    ]
    copies = [load_cur] + [
        pltpu.make_async_copy(source, target, load_sem.at[i])
        for i, (source, target) in enumerate(loads, 1)
    ]
    for copy in copies[1:]:
        copy.start()
    blk_copies = [
        pltpu.make_async_copy(
            blocks.at[pl.ds(i * CHUNK, CHUNK)], near_blk.at[pl.ds(i * CHUNK, CHUNK)], blk_sem.at[i]
        )
        for i in range(CHUNKS)
    ]
    for copy in blk_copies:
        copy.start()

    load_cur.wait()
    own_cur = [cur_v[:, c, :] for c in range(2)]
    for c in range(2):
        near_cur[1, c] = own_cur[c].astype(BF16)
    cur_msg[me] = message(own_cur)

    def clear(near_slot, up_slot):
        if near_slot is not None:
            near_cur[near_slot] = jnp.zeros((2, LEAF, 128), BF16)
        if up_slot is not None:
            up_msg[up_slot] = jnp.zeros((2 * PAR + 16, 128), jnp.int16)

    pl.when(jnp.logical_not(has_before))(functools.partial(clear, 0, None))
    pl.when(jnp.logical_not(has_after))(functools.partial(clear, 2, None))
    pl.when(jnp.logical_not(has_down))(functools.partial(clear, None, 0))
    pl.when(jnp.logical_not(has_up))(functools.partial(clear, None, 2))
    pl.semaphore_wait(barrier, greeted)

    def called(there, semaphore, where):
        @pl.when(there)
        def call():
            pl.semaphore_signal(semaphore, inc=1, device_id=where, device_id_type=MESH)

    called(late, up_greet, up_id)
    called(near_late, near_greet, after_id)
    near_out = [
        pltpu.make_async_remote_copy(
            src_ref=near_cur.at[1],
            dst_ref=near_cur.at[slot],
            send_sem=near_send.at[i],
            recv_sem=near_recv.at[i],
            device_id=where,
            device_id_type=MESH,
        )
        for i, (slot, where) in enumerate(((0, after_id), (2, before_id)))
    ]
    cur_out = [
        pltpu.make_async_remote_copy(
            src_ref=cur_msg.at[me],
            dst_ref=cur_msg.at[me],
            send_sem=cur_send.at[o - 1],
            recv_sem=cur_recv.at[o - 1],
            device_id=peers[o],
            device_id_type=MESH,
        )
        for o in ORDER
    ]
    for copy in cur_out:
        copy.start()
    across = (has_after & (me == SMP - 1), has_before & (me == 0) & jnp.logical_not(near_defers))
    for copy, there in zip(near_out, across):
        pl.when(there)(copy.start)

    for copy in copies[1:9]:
        copy.wait()
    grid = itp_v[...]
    both = mm(split3(rad_v[...].reshape(256, 256)), stacked(grid))
    m_op[...] = stacked(complex_square(both[:128], both[128:]))
    both = mm(grid, jnp.concatenate([rec_v[0], rec_v[1]], axis=1), TN, HIGHEST)
    n_op[...] = stacked(complex_square(both[:, :128], both[:, 128:]))
    angles = ph_v[...]
    table = jnp.concatenate([jnp.cos(angles), jnp.sin(angles)], axis=1)
    position = (oc_v[...] == iota((8, GROUP), 0)).astype(F32)
    shift[...] = mm(position, table, TN, HIGHEST)
    owner = pm_v[...]
    member = (owner == iota((PAR, GROUP), 0)).astype(BF16)
    to_parent[...] = jnp.concatenate([member, member], axis=1)
    member = (owner == (iota((PAR, GROUP), 0) ^ 7)).astype(F32)
    to_leaf[...] = jnp.concatenate([member, member], axis=0).T.astype(BF16)
    masks = far_masks(fs_v[...] - (clu - 1) * PAR)
    for q in range(WORDS):
        words[q] = jnp.broadcast_to(masks[:, 4 * q : 4 * q + 1], (PAR, 128))
    copies[9].wait()
    copies[10].wait()
    t_re[...] = tr_v[:, 0, :]
    t_minus[...] = tr_v[:, 1, :] - tr_v[:, 0, :]
    t_plus[...] = tr_v[:, 1, :] + tr_v[:, 0, :]

    lane_leaf = lax.rem(iota((128, 128), 1), LEAF)

    def near_chunk(i, carry):
        first = pl.multiple_of(i * CHUNK, CHUNK)
        pltpu.make_async_copy(
            blocks.at[pl.ds(first, CHUNK)], near_blk.at[pl.ds(first, CHUNK)], blk_sem.at[i]
        ).wait()
        lhs = jnp.concatenate(
            [
                near_blk[pl.ds(first, CHUNK), s, c].reshape(CHUNK * 128, 128)
                for s in range(SLOTS)
                for c in range(2)
            ],
            axis=1,
        )
        result = mm(lhs, near_x[...])
        total = near_acc[...]
        for r in range(CHUNK):
            total = jnp.where(lane_leaf == first + r, result[r * 128 : (r + 1) * 128], total)
        near_acc[...] = total
        return carry

    for copy in cur_out:
        copy.wait_recv()
    x = jnp.concatenate(
        [jnp.concatenate(decoded(cur_msg[i], LEAF), axis=1) for i in range(SMP)], axis=0
    )
    inter = mm(split3(x), m_op[...])
    cos, sin = shift[:, :128], shift[:, 128:]
    real, imag = inter[:, :128], inter[:, 128:]
    shifted = jnp.concatenate([real * cos - imag * sin, real * sin + imag * cos], axis=1)
    own = mm(to_parent[...], jnp.concatenate(halves(shifted), axis=0))
    own = [own[:, :128], own[:, 128:]]
    for c in range(2):
        upper[1, c] = own[c]
    up_msg[1] = message(own)
    up_out = [
        pltpu.make_async_remote_copy(
            src_ref=up_msg.at[1],
            dst_ref=up_msg.at[slot],
            send_sem=up_send.at[i],
            recv_sem=up_recv.at[i],
            device_id=where,
            device_id_type=MESH,
        )
        for i, (slot, where) in enumerate(((0, up_id), (2, down_id)))
    ]
    pl.when(has_up)(up_out[0].start)

    @pl.when(defers)
    def await_late():
        pl.semaphore_wait(up_greet, 1)

    pl.when(has_down)(up_out[1].start)

    for copy, there in zip(near_out, (me < SMP - 1, me > 0)):
        pl.when(there)(copy.start)

    @pl.when(near_defers)
    def await_near_late():
        pl.semaphore_wait(near_greet, 1)
        near_out[1].start()

    def translate(group):
        def octet_step(step, sums):
            sums = list(sums)
            start = pl.multiple_of(8 * step, 8)
            up_re = upper[group, 0, pl.ds(start, 8)]
            up_im = upper[group, 1, pl.ds(start, 8)]
            offset = jnp.full((8, 128), 8 * lax.rem(step, 4), I32)
            word = 3 * group + step // 4
            marks = [
                lax.shift_right_logical(words[word, 8 * b : 8 * b + 8], offset)
                for b in range(BLOCKS)
            ]
            for i in range(8):
                source_re = jnp.broadcast_to(up_re[i : i + 1], (8, 128))
                source_im = jnp.broadcast_to(up_im[i : i + 1], (8, 128))
                source_sum = source_re + source_im
                for b in range(BLOCKS):
                    at = PAR * group + start + (89 + i - 8 * b)
                    op_re = t_re[pl.ds(at, 8)]
                    op_minus = t_minus[pl.ds(at, 8)]
                    op_plus = t_plus[pl.ds(at, 8)]
                    there = (marks[b] & (1 << i)) != 0
                    here_re = jnp.where(there, source_re, 0.0)
                    here_im = jnp.where(there, source_im, 0.0)
                    here_sum = jnp.where(there, source_sum, 0.0)
                    sums[3 * b] = sums[3 * b] + op_re * here_sum
                    sums[3 * b + 1] = sums[3 * b + 1] + op_minus * here_re
                    sums[3 * b + 2] = sums[3 * b + 2] + op_plus * here_im
            return tuple(sums)

        sums = tuple(jnp.zeros((8, 128), F32) for _ in range(3 * BLOCKS))
        def octet_pair(pair, sums):
            return octet_step(2 * pair + 1, octet_step(2 * pair, sums))

        sums = lax.fori_loop(0, BLOCKS // 2, octet_pair, sums)
        for b in range(BLOCKS):
            both, minus, plus = sums[3 * b : 3 * b + 3]
            for c, value in enumerate((both - plus, both + minus)):
                place = (pl.ds(8 * b, 8), pl.ds(128 * c, 128))
                incoming[place] = incoming[place] + value

    part_out = [
        pltpu.make_async_remote_copy(
            src_ref=part_msg.at[lax.rem(me + o, SMP)],
            dst_ref=arrived.at[o - 1],
            send_sem=part_send.at[o - 1],
            recv_sem=part_recv.at[o - 1],
            device_id=peers[o],
            device_id_type=MESH,
        )
        for o in ORDER
    ]

    def spread():
        field = mm(to_leaf[...], jnp.concatenate(halves(incoming[...]), axis=0))
        cos, sin = shift[:, :128], shift[:, 128:]
        real, imag = field[:, :128], field[:, 128:]
        back = jnp.concatenate([real * cos + imag * sin, imag * cos - real * sin], axis=1)
        result = mm(split3(back), n_op[...])
        part[...] = result.reshape(SMP, LEAF, 256)
        for i in range(SMP):
            rows = result[i * LEAF : (i + 1) * LEAF]
            part_msg[i] = message([rows[:, :128], rows[:, 128:]])
        for copy in part_out:
            copy.start()

    incoming[...] = jnp.zeros((PAR, 256), F32)
    near_acc[...] = jnp.zeros((128, 128), F32)

    def near_sides():
        for copy, there in zip(near_out, (has_before, has_after)):
            pl.when(there)(copy.wait_recv)
        p_re = near_cur[:, 0].reshape(PAR, 128).astype(F32)
        p_im = near_cur[:, 1].reshape(PAR, 128).astype(F32)
        sources = jnp.concatenate(
            [jnp.concatenate([p_re, -p_im], axis=1), jnp.concatenate([p_im, p_re], axis=1)], axis=0
        )
        local = ns_v[...] - (device - 1) * LEAF
        local = jnp.concatenate(
            [local, local + PAR, jnp.full((SLOTS, 64), -1, I32)], axis=1
        )
        rows = iota((2 * PAR, 128), 0)
        picks = jnp.concatenate(
            [(local[s : s + 1] == rows).astype(F32) for s in range(SLOTS)], axis=1
        ).astype(BF16)
        rhs = mm(sources.T.astype(BF16), picks).astype(BF16)
        for s in range(SLOTS):
            near_x[pl.ds(s * 256, 256)] = rhs[:, s * 128 : (s + 1) * 128]

    order = jnp.where(lax.rem(clu, 4) == 0, 1, 2)

    ahead = jnp.where(lax.rem(clu, 4) == 0, EARLY, 0)
    sides_at = jnp.where(lax.rem(clu, 4) == 0, 0, 2)

    def phase(turn, carry):
        group = lax.rem(1 + order * turn, 3)
        pl.when((group == 0) & has_down)(up_out[0].wait_recv)
        pl.when((group == 2) & has_up)(up_out[1].wait_recv)
        missing = ((group == 0) & jnp.logical_not(has_down)) | (
            (group == 2) & jnp.logical_not(has_up)
        )

        @pl.when(turn > 0)
        def take():
            for c, value in enumerate(decoded(up_msg[group], PAR)):
                upper[group, c] = value

        pl.when(jnp.logical_not(missing))(functools.partial(translate, group))
        pl.when(turn == 2)(spread)
        pl.when(turn == sides_at)(near_sides)
        lax.fori_loop(
            jnp.where(turn == 0, 0, ahead),
            jnp.where(turn == 2, CHUNKS, ahead),
            near_chunk,
            0,
        )
        return carry

    lax.fori_loop(0, 3, phase, 0)

    near = near_acc[...].T
    total = part[me] + jnp.concatenate([near[:LEAF], near[LEAF : 2 * LEAF]], axis=1)
    for copy, o in zip(part_out, ORDER):
        copy.wait_recv()
        total = total + jnp.concatenate(decoded(arrived[o - 1], LEAF), axis=1)
    out[:, 0, :] = total[:, :128]
    out[:, 1, :] = total[:, 128:]
    for copy, there in zip((*near_out, *up_out), (has_after, has_before, has_up, has_down)):
        pl.when(there)(copy.wait_send)
    for copy in (*cur_out, *part_out):
        copy.wait_send()


def on_device(
    currents,
    near_blocks,
    near_src,
    radiation,
    interp,
    shift_phase,
    parent_map,
    octant,
    trans,
    far_src,
    far_kind,
    receive,
):
    hbm_spec = pl.BlockSpec(memory_space=pltpu.HBM)
    vmem = pltpu.VMEM
    dma = pltpu.SemaphoreType.DMA
    return pl.pallas_call(
        body,
        out_shape=vmem((LEAF, 2, 128), F32),
        in_specs=[hbm_spec] * 11,
        out_specs=pl.BlockSpec(memory_space=vmem),
        scratch_shapes=[
            vmem((LEAF, 2, 128), F32),
            vmem((SMP, 2 * LEAF + 16, 128), jnp.int16),
            vmem((3, 2, LEAF, 128), BF16),
            vmem((LEAF, SLOTS, 2, 128, 128), BF16),
            vmem((SLOTS, LEAF), I32),
            vmem((2, 128, 256), F32),
            vmem((256, 128), F32),
            vmem((8, 128), F32),
            vmem((1, GROUP), I32),
            vmem((1, GROUP), I32),
            vmem((TABLE, 2, 128), F32),
            vmem((64, PAR), I32),
            vmem((2, 256, 128), F32),
            vmem((TABLE, 128), F32),
            vmem((TABLE, 128), F32),
            vmem((TABLE, 128), F32),
            vmem((3, 2, PAR, 128), F32),
            vmem((3, 2 * PAR + 16, 128), jnp.int16),
            vmem((768, 256), BF16),
            vmem((768, 256), BF16),
            vmem((GROUP, 256), F32),
            vmem((PAR, 512), BF16),
            vmem((GROUP, 192), BF16),
            vmem((WORDS, PAR, 128), I32),
            vmem((SLOTS * 256, 128), BF16),
            vmem((128, 128), F32),
            vmem((PAR, 256), F32),
            vmem((SMP, LEAF, 256), F32),
            vmem((SMP, 2 * LEAF + 16, 128), jnp.int16),
            vmem((SMP - 1, 2 * LEAF + 16, 128), jnp.int16),
            dma((11,)),
            dma((CHUNKS,)),
            dma((2,)),
            dma((2,)),
            dma((SMP - 1,)),
            dma((SMP - 1,)),
            dma((2,)),
            dma((2,)),
            dma((SMP - 1,)),
            dma((SMP - 1,)),
            pltpu.SemaphoreType.REGULAR,
            pltpu.SemaphoreType.REGULAR,
        ],
        compiler_params=pltpu.CompilerParams(
            collective_id=0, has_side_effects=True, vmem_limit_bytes=60 * 1024 * 1024
        ),
        name="far_and_near",
    )(
        currents,
        near_blocks,
        near_src.T,
        radiation,
        interp,
        shift_phase,
        parent_map,
        octant,
        trans,
        far_src.T,
        receive,
    )


def solution(mesh):
    in_specs = (
        P(("clu", "smp"), None, None),
        P(("clu", "smp"), None, None, None, None),
        P(("clu", "smp"), None),
        P(),
        P(),
        P(),
        P("clu", None),
        P("clu", None),
        P(None, None, "smp"),
        P("clu", None),
        P("clu", None),
        P(),
    )
    out_specs = P(("clu", "smp"), None, None)
    return jax.shard_map(
        on_device, mesh=mesh, in_specs=in_specs, out_specs=out_specs, check_vma=False
    )
```
